32 devices in a mesh: scene: 2 (over core), seq: 16 (over z, y, x).
Axes of the slice: x: 2, y: 2, z: 4, core: 2. Of those that a mesh axis runs over, the one named last changes fastest.
Arguments:
- points: bfloat16 [131072, 512], P(('scene', 'seq')), parts along dimension 0, may hold values from -6 to 6
- order: int32 [1024], P(('scene', 'seq')), parts along dimension 0, may hold values from 0 to 511, as said below
- offsets: int32 [128], P(('scene', 'seq')), parts along dimension 0, may hold values from -2 to 2, as said below
- norm_gain: float32 [512], replicated, may hold values from 0.25 to 1.75
- w_qkv: bfloat16 [512, 1536], replicated, may hold values from -8 to 8
- w_out: bfloat16 [512, 512], replicated, may hold values from -0.25 to 0.25
Outputs:
- mixed: bfloat16 [131072, 512], P(('scene', 'seq')), parts along dimension 0
The draws below stay inside these ranges and needn't reach their ends.
There are 2 independent parts, one for each index of `scene`. The reference program is written for one: setup_inputs(seed, part) draws one part's arguments, and reference() takes and returns one part's arrays. A program takes and returns all parts, laid end to end along the dimension named above; an argument that names none is the same for every part. Nothing has to cross between parts.
Inputs may be any that keep to these rules, and one draw needn't show every extreme that they name: `order`: a permutation of 0 to 511; among the blocks of one device at most 2 take serial positions in one range e * 32 to (e + 1) * 32 - 1, and some device has exactly 2 in one such range. `offsets`: never zero; both minus 2 and 2 occur.
All inputs are finite; a program needn't handle non-finite values.
Results may differ from the reference program's by a relative error of at most 0.0049.
Values may be sent and summed in bfloat16 or wider, within the bound.
No kernel may reach another device: no remote copies, remote signals or barrier semaphores. Data moves between devices by JAX's collectives and lax.ppermute only.
A program may use at most 192 MiB of HBM per device.

```python
import math
import jax
import jax.numpy as jnp
from jax import lax

D = 512
HEADS = 8
BLOCK = 128
PATCH = 1024
REACH = 2
BLK_DEV = 32
BLOCKS = 512
POINTS = 65536
PATCHES = 64
CAP = 2
N_SEQ = 16


def draw_order(key, part):
    key = jax.random.fold_in(key, 11)
    subkeys = jax.random.split(key, 5)
    total = N_SEQ * BLK_DEV
    alpha = jax.random.permutation(subkeys[0], N_SEQ)
    beta = jax.random.permutation(subkeys[1], N_SEQ)
    shifts = jnp.tile(jax.random.permutation(subkeys[2], N_SEQ), CAP)[:BLK_DEV]
    scores = jax.random.randint(subkeys[3], (N_SEQ, BLK_DEV), 0, 4096) * BLK_DEV + jnp.arange(BLK_DEV)[None, :]
    shuffle = jnp.argsort(scores, axis=1, stable=True)
    target = alpha[(beta[:, None] + shifts[shuffle]) % N_SEQ].reshape(-1)
    ties = jax.random.permutation(subkeys[4], total)
    ranked = jnp.argsort(target * total + ties, stable=True)
    return jnp.zeros((total,), jnp.int32).at[ranked].set(jnp.arange(total, dtype=jnp.int32))


def draw_offsets(key, part):
    key = jax.random.fold_in(key, 17)
    subkeys = jax.random.split(key, 4)
    magnitude = jax.random.randint(subkeys[0], (PATCHES,), 1, REACH + 1)
    signs = jax.random.randint(subkeys[1], (PATCHES,), 0, 2) * 2 - 1
    result = (magnitude * signs).astype(jnp.int32)
    first = jax.random.randint(subkeys[2], (), 0, PATCHES)
    second = (first + 1 + jax.random.randint(subkeys[3], (), 0, PATCHES - 1)) % PATCHES
    return result.at[first].set(0 - REACH).at[second].set(REACH)


def draw_w_qkv(key, part):
    key = jax.random.fold_in(key, 23)
    base = jnp.clip(jax.random.normal(key, (D, 3 * D), jnp.float32), -4.0, 4.0) * D ** (-0.5)
    return base.astype(jnp.bfloat16)


def steps_of(stream_key, shape, pieces, least, largest):
    level = 1.0
    for axis_at, blocks in pieces:
        steps = jax.random.uniform(jax.random.fold_in(jax.random.fold_in(stream_key, 6), axis_at), (blocks,), jnp.float32, least / len(pieces), largest / len(pieces))
        level = level * jnp.repeat(jnp.exp(steps), shape[axis_at] // blocks).reshape((-1,) + (1,) * (len(shape) - 1 - axis_at))
    return level


def bell_draw(own_key, shape, width, most, shards=(), held_as=jnp.bfloat16):
    factor_of = steps_of(own_key, shape, shards, -0.22, 0.18) if shards else 1.0
    entries = jax.random.normal(own_key, shape, jnp.float32) * width * factor_of
    return jnp.minimum(jnp.maximum(entries, -most), most).astype(held_as)


def setup_inputs(seed: int = 0, part: int = 0) -> dict:
    seeds = jax.random.split(jax.random.key(seed), 7)
    part_splits = jax.random.split(jax.random.fold_in(seeds[6], part), 7)
    points = bell_draw(part_splits[0], (POINTS, D), 1.0, 6.0, ((0, 16),))
    order = draw_order(jax.random.fold_in(jax.random.fold_in(seeds[6], part), 71), part)
    offsets = draw_offsets(jax.random.fold_in(jax.random.fold_in(seeds[6], part), 71), part)
    norm_gain = jnp.clip(1.0 + 0.15 * jax.random.normal(seeds[3], (D,), jnp.float32), 0.25, 1.75)
    w_qkv = draw_w_qkv(jax.random.fold_in(seeds[6], 71), part)
    w_out = bell_draw(seeds[5], (D, D), D ** -0.5, 0.25)
    return {"points": points, "order": order, "offsets": offsets, "norm_gain": norm_gain, "w_qkv": w_qkv, "w_out": w_out}


def layer_norm(row_block, norm_gain):
    values = row_block.astype(jnp.float32)
    centre = lax.optimization_barrier(jnp.mean(values, axis=-1, keepdims=True))
    spread = lax.optimization_barrier(jnp.mean(jnp.square(values - centre), axis=-1, keepdims=True))
    return ((values - centre) * lax.rsqrt(spread + 1e-05) * norm_gain).astype(jnp.bfloat16)

def attend_one(operands):
    queries, key_block, value_block = operands
    scores = jnp.dot(queries, key_block.T, preferred_element_type=jnp.float32) / math.sqrt(queries.shape[-1])
    row_max = lax.optimization_barrier(jnp.max(scores, axis=-1, keepdims=True))
    raised = jnp.exp(scores - row_max)
    weights = (raised / lax.optimization_barrier(jnp.sum(raised, axis=-1, keepdims=True))).astype(jnp.bfloat16)
    return jnp.dot(weights, value_block, preferred_element_type=jnp.float32).astype(jnp.bfloat16)

def heads_first(row_block, head_count):
    total, length, features = row_block.shape
    split = row_block.reshape(total, length, head_count, features // head_count)
    return split.transpose(0, 2, 1, 3).reshape(total * head_count, length, features // head_count)

def patch_attention(queries, key_sets, value_sets, head_count):
    total, length, features = queries.shape
    result = lax.map(attend_one, (heads_first(queries, head_count), heads_first(key_sets, head_count), heads_first(value_sets, head_count)))
    result = result.reshape(total, head_count, length, features // head_count)
    return result.transpose(0, 2, 1, 3).reshape(total * length, features)

def reference(points, order, offsets, norm_gain, w_qkv, w_out):
    blocks = points.reshape(BLOCKS, BLOCK, D)
    serial = blocks[jnp.argsort(order)].reshape(POINTS, D)
    normed = layer_norm(serial, norm_gain)
    projected = jnp.dot(normed, w_qkv, preferred_element_type=jnp.float32).astype(jnp.bfloat16)
    patched = projected.reshape(PATCHES, PATCH, 3 * D)
    partner_index = (jnp.arange(PATCHES, dtype=jnp.int32) + offsets.astype(jnp.int32)) % PATCHES
    partner = patched[partner_index]
    key_sets = jnp.concatenate([patched[:, :, D:2 * D], partner[:, :, D:2 * D]], axis=1)
    value_sets = jnp.concatenate([patched[:, :, 2 * D:], partner[:, :, 2 * D:]], axis=1)
    attended = patch_attention(patched[:, :, :D], key_sets, value_sets, HEADS)
    serial_out = (serial.astype(jnp.float32) + jnp.dot(attended, w_out, preferred_element_type=jnp.float32)).astype(jnp.bfloat16)
    return serial_out.reshape(BLOCKS, BLOCK, D)[order].reshape(POINTS, D)
```

```python
import functools
import math

import jax
import jax.numpy as jnp
from jax import lax
from jax.experimental import pallas as pl
from jax.experimental.pallas import tpu as pltpu
from jax.sharding import PartitionSpec as P

HEADS = 8
REACH = 2
KEY_TILE = 512
QUERY_TILE = 256
ONES_ROWS = 16
SAFE_SCORE = 80.0
VMEM_BYTES = 56 * 1024 * 1024
BF = jnp.bfloat16
F32 = jnp.float32


def ring_order(count):
    grids = {16: (4, 2, 2), 64: (4, 4, 4)}
    if count not in grids:
        return list(range(count))
    deep, tall, wide = grids[count]
    columns = [(0, x) for x in range(wide)]
    for y in range(1, tall):
        across = range(wide - 1, 0, -1) if y % 2 else range(1, wide)
        columns += [(y, x) for x in across]
    columns += [(y, 0) for y in range(tall - 1, 0, -1)]
    ring = []
    for at, (y, x) in enumerate(columns):
        along = range(deep) if at % 2 == 0 else range(deep - 1, -1, -1)
        ring += [(z * tall + y) * wide + x for z in along]
    return ring


def params(**more):
    return pltpu.CompilerParams(vmem_limit_bytes=VMEM_BYTES, **more)


def moved_blocks(source, index, name):
    count = index.shape[0]

    def kernel(index_ref, source_ref, out_ref, sems):
        copies = [
            pltpu.make_async_copy(source_ref.at[index_ref[i]], out_ref.at[i], sems.at[i]) for i in range(count)
        ]
        for copy in copies:
            copy.start()
        for copy in copies:
            copy.wait()

    return pl.pallas_call(
        kernel,
        grid_spec=pltpu.PrefetchScalarGridSpec(
            num_scalar_prefetch=1,
            grid=(1,),
            in_specs=[pl.BlockSpec(memory_space=pl.ANY)],
            out_specs=pl.BlockSpec(memory_space=pl.ANY),
            scratch_shapes=[pltpu.SemaphoreType.DMA((count,))],
        ),
        out_shape=jax.ShapeDtypeStruct((count,) + source.shape[1:], source.dtype),
        name=name,
    )(index, source)


def norm_kernel(picked_ref, *refs):
    *block_refs, gain_ref, low_ref, high_ref = refs
    patch = pl.program_id(0)
    half = pl.num_programs(0) // 2

    def write(out_ref):
        for i, block_ref in enumerate(block_refs):
            length = block_ref.shape[1]
            values = block_ref[0].astype(F32)
            centred = values - jnp.mean(values, axis=-1, keepdims=True)
            spread = jnp.mean(jnp.square(centred), axis=-1, keepdims=True)
            out_ref[i * length : (i + 1) * length, :] = (
                centred * lax.rsqrt(spread + 1e-05) * gain_ref[...]
            ).astype(BF)

    @pl.when(patch < half)
    def _():
        write(low_ref)

    @pl.when(patch >= half)
    def _():
        write(high_ref)


def normed_patches(arrived, picked, norm_gain, patch_count):
    _, length, features = arrived.shape
    per_patch = picked.shape[0] // patch_count
    half = patch_count // 2
    rows = per_patch * length

    def block_spec(i):
        return pl.BlockSpec((1, length, features), lambda p, s: (s[p * per_patch + i], 0, 0))

    return pl.pallas_call(
        norm_kernel,
        grid_spec=pltpu.PrefetchScalarGridSpec(
            num_scalar_prefetch=1,
            grid=(patch_count,),
            in_specs=[block_spec(i) for i in range(per_patch)] + [pl.BlockSpec((1, features), lambda p, s: (0, 0))],
            out_specs=[
                pl.BlockSpec((rows, features), lambda p, s: (jnp.minimum(p, half - 1), 0)),
                pl.BlockSpec((rows, features), lambda p, s: (jnp.maximum(p - half, 0), 0)),
            ],
        ),
        out_shape=[jax.ShapeDtypeStruct((half * rows, features), BF)] * 2,
        compiler_params=params(),
        name="norm",
    )(picked, *([arrived] * per_patch), norm_gain.reshape(1, features))


def nt_dot(a, b):
    return lax.dot_general(a, b, (((1,), (1,)), ((), ())), preferred_element_type=F32)


def squares_of_keys(keys, width):
    features = keys.shape[1]
    head = lax.broadcasted_iota(jnp.int32, (features, 128), 0) // width
    column = lax.broadcasted_iota(jnp.int32, (features, 128), 1)
    member = jnp.where(head == column, 1.0, 0.0).astype(BF)
    squared = jnp.square(keys.astype(F32)).astype(BF)
    return jnp.max(jnp.dot(squared, member, preferred_element_type=F32))


def squares_of_queries(queries, width):
    features, count = queries.shape
    squared = jnp.square(queries.astype(F32)).reshape(features // width, width, count)
    return jnp.max(jnp.sum(squared, axis=1))


def lone_head(pair, which, width):
    kept = pair[which * width : (which + 1) * width]
    blank = jnp.zeros_like(kept)
    return jnp.concatenate([kept, blank] if which == 0 else [blank, kept], axis=0)


def with_ones(values):
    return jnp.concatenate([values, jnp.ones((ONES_ROWS, values.shape[1]), BF)], axis=0)


def plain_head(query_ref, key_ref, value_ref, head, width):
    pair = 2 * width * (head // 2)
    query = lone_head(query_ref[pair : pair + 2 * width, :], head % 2, width)
    total = None
    for at in range(0, key_ref.shape[0], KEY_TILE):
        scores = jnp.dot(key_ref[at : at + KEY_TILE, pair : pair + 2 * width], query, preferred_element_type=F32)
        raised = jnp.exp2(scores).astype(BF)
        values = with_ones(value_ref[head * width : (head + 1) * width, at : at + KEY_TILE])
        part = jnp.dot(values, raised, preferred_element_type=F32)
        total = part if total is None else total + part
    return total


def shifted_heads(query_ref, key_ref, value_ref, width, use):
    head_count = key_ref.shape[1] // width
    tiles = query_ref.shape[1] // QUERY_TILE

    def one(step, carry):
        pair, tile = step // tiles, step % tiles
        features = pl.ds(pl.multiple_of(pair * 2 * width, 2 * width), 2 * width)
        columns = pl.ds(pl.multiple_of(tile * QUERY_TILE, QUERY_TILE), QUERY_TILE)
        queries = query_ref[features, columns]
        keys = key_ref[:, features]
        for which in range(2):
            scores = jnp.dot(keys, lone_head(queries, which, width), preferred_element_type=F32)
            top = jnp.max(scores, axis=0, keepdims=True)
            raised = jnp.exp2(scores - top).astype(BF)
            rows = pl.ds(pl.multiple_of(pair * 2 * width + which * width, width), width)
            sums = jnp.dot(with_ones(value_ref[rows, :]), raised, preferred_element_type=F32)
            use(rows, pair * 2 + which, columns, top, sums)
        return carry

    lax.fori_loop(0, head_count // 2 * tiles, one, 0)


def own_kernel(low_ref, high_ref, wk_ref, wqv_ref, query_ref, total_ref, mass_ref, top_ref, key_s, value_s, *, width):
    patch = pl.program_id(0)
    half = pl.num_programs(0) // 2
    features = wk_ref.shape[0]

    def project(normed_ref):
        normed = normed_ref[...]
        key_s[...] = jnp.dot(normed, wk_ref[...], preferred_element_type=F32).astype(BF)
        both = nt_dot(wqv_ref[...], normed)
        query_ref[...] = (both[:features] * (math.log2(math.e) / math.sqrt(width))).astype(BF)
        value_s[...] = both[features:].astype(BF)

    @pl.when(patch < half)
    def _():
        project(low_ref)

    @pl.when(patch >= half)
    def _():
        project(high_ref)

    bound = squares_of_queries(query_ref[...], width) * squares_of_keys(key_s[...], width)
    small = bound < SAFE_SCORE * SAFE_SCORE

    @pl.when(small)
    def _():
        for head in range(features // width):
            sums = plain_head(query_ref, key_s, value_s, head, width)
            total_ref[head * width : (head + 1) * width, :] = sums[:width]
            mass_ref[head : head + 1, :] = sums[width : width + 1]
        top_ref[...] = jnp.zeros_like(top_ref)

    @pl.when(jnp.logical_not(small))
    def _():
        def use(rows, head, columns, top, sums):
            total_ref[rows, columns] = sums[:width]
            mass_ref[pl.ds(head, 1), columns] = sums[width : width + 1]
            top_ref[pl.ds(head, 1), columns] = top

        shifted_heads(query_ref, key_s, value_s, width, use)


def own_attention(low, high, wk, wqv, patch_count):
    features = wk.shape[0]
    half = patch_count // 2
    rows = low.shape[0] // half
    width = features // HEADS
    whole = lambda p: (0, 0)
    along = lambda p: (0, p)
    return pl.pallas_call(
        functools.partial(own_kernel, width=width),
        grid=(patch_count,),
        in_specs=[
            pl.BlockSpec((rows, features), lambda p: (jnp.minimum(p, half - 1), 0)),
            pl.BlockSpec((rows, features), lambda p: (jnp.maximum(p - half, 0), 0)),
            pl.BlockSpec(wk.shape, whole),
            pl.BlockSpec(wqv.shape, whole),
        ],
        out_specs=[
            pl.BlockSpec((features, rows), along),
            pl.BlockSpec((features, rows), along),
            pl.BlockSpec((HEADS, rows), along),
            pl.BlockSpec((HEADS, rows), along),
        ],
        out_shape=[
            jax.ShapeDtypeStruct((features, patch_count * rows), BF),
            jax.ShapeDtypeStruct((features, patch_count * rows), F32),
            jax.ShapeDtypeStruct((HEADS, patch_count * rows), F32),
            jax.ShapeDtypeStruct((HEADS, patch_count * rows), F32),
        ],
        scratch_shapes=[pltpu.VMEM((rows, features), BF), pltpu.VMEM((features, rows), BF)],
        compiler_params=params(),
        cost_estimate=pl.CostEstimate(flops=40 * 10**9, bytes_accessed=28 * 10**6, transcendentals=0),
        name="own",
    )(low, high, wk, wqv)


def partner_kernel(
    picked_ref,
    source_ref,
    within_ref,
    left_ref,
    low_ref,
    high_ref,
    right_ref,
    query_ref,
    total_ref,
    mass_ref,
    top_ref,
    wk_ref,
    wv_ref,
    wo_ref,
    arrived_ref,
    out_ref,
    normed_s,
    key_s,
    value_s,
    mixed_s,
    *,
    width,
):
    patch = pl.program_id(0)
    features = wk_ref.shape[0]
    for number, normed_ref in enumerate((left_ref, low_ref, high_ref, right_ref)):

        @pl.when(source_ref[patch] == number)
        def _(normed_ref=normed_ref):
            normed_s[...] = normed_ref[...]

    normed = normed_s[...]
    key_s[...] = jnp.dot(normed, wk_ref[...], preferred_element_type=F32).astype(BF)
    value_s[...] = nt_dot(wv_ref[...], normed).astype(BF)
    bound = squares_of_queries(query_ref[...], width) * squares_of_keys(key_s[...], width)
    unshifted = jnp.max(jnp.abs(top_ref[...])) == 0.0
    small = jnp.logical_and(bound < SAFE_SCORE * SAFE_SCORE, unshifted)

    @pl.when(small)
    def _():
        for head in range(features // width):
            sums = plain_head(query_ref, key_s, value_s, head, width)
            rows = slice(head * width, (head + 1) * width)
            mass = mass_ref[head : head + 1, :] + sums[width : width + 1]
            mixed_s[rows, :] = ((total_ref[rows, :] + sums[:width]) / mass).astype(BF)

    @pl.when(jnp.logical_not(small))
    def _():
        def use(rows, head, columns, top, sums):
            one = pl.ds(head, 1)
            before = top_ref[one, columns]
            highest = jnp.maximum(before, top)
            mine, theirs = jnp.exp2(before - highest), jnp.exp2(top - highest)
            mass = mass_ref[one, columns] * mine + sums[width : width + 1] * theirs
            mixed_s[rows, columns] = ((total_ref[rows, columns] * mine + sums[:width] * theirs) / mass).astype(BF)

        shifted_heads(query_ref, key_s, value_s, width, use)

    length = arrived_ref.shape[1]
    per_patch = mixed_s.shape[1] // length
    mixed = lax.dot_general(mixed_s[...], wo_ref[...], (((0,), (0,)), ((), ())), preferred_element_type=F32)
    for i in range(per_patch):
        slot = picked_ref[patch * per_patch + i]
        out_ref[slot] = (arrived_ref[slot].astype(F32) + mixed[i * length : (i + 1) * length]).astype(BF)


def partner_attention(picked, source, within, sets, query, total, mass, top, wk, wv, wo, arrived):
    features = wk.shape[0]
    patch_count = source.shape[0]
    rows = query.shape[1] // patch_count
    whole = lambda p, *s: (0, 0)
    whole3 = lambda p, *s: (0, 0, 0)
    along = lambda p, *s: (0, p)

    def set_spec(number):
        return pl.BlockSpec((rows, features), lambda p, k, s, w: (jnp.where(s[p] == number, w[p], 0), 0))

    return pl.pallas_call(
        functools.partial(partner_kernel, width=features // HEADS),
        grid_spec=pltpu.PrefetchScalarGridSpec(
            num_scalar_prefetch=3,
            grid=(patch_count,),
            in_specs=[set_spec(number) for number in range(4)]
            + [
                pl.BlockSpec((features, rows), along),
                pl.BlockSpec((features, rows), along),
                pl.BlockSpec((HEADS, rows), along),
                pl.BlockSpec((HEADS, rows), along),
                pl.BlockSpec(wk.shape, whole),
                pl.BlockSpec(wv.shape, whole),
                pl.BlockSpec(wo.shape, whole),
                pl.BlockSpec(arrived.shape, whole3),
            ],
            out_specs=pl.BlockSpec(arrived.shape, whole3),
            scratch_shapes=[
                pltpu.VMEM((rows, features), BF),
                pltpu.VMEM((rows, features), BF),
                pltpu.VMEM((features, rows), BF),
                pltpu.VMEM((features, rows), BF),
            ],
        ),
        out_shape=jax.ShapeDtypeStruct(arrived.shape, BF),
        compiler_params=params(),
        cost_estimate=pl.CostEstimate(flops=40 * 10**9, bytes_accessed=28 * 10**6, transcendentals=0),
        name="partner",
    )(picked, source, within, *sets, query, total, mass, top, wk, wv, wo, arrived)


def body(points, order, offsets, norm_gain, w_qkv, w_out):
    features = points.shape[1]
    block_count = order.shape[0]
    block_rows = points.shape[0] // block_count
    patch_count = offsets.shape[0]
    shards = lax.axis_size("seq")
    capacity = (block_count + shards - 1) // shards
    ring = ring_order(shards)
    ring_next = [(ring[e], ring[(e + 1) % shards]) for e in range(shards)]
    ring_before = [(ring[e], ring[e - 1]) for e in range(shards)]
    places = jnp.asarray(ring, jnp.int32)

    block_ids = jnp.arange(block_count, dtype=jnp.int32)
    shard_ids = jnp.arange(shards, dtype=jnp.int32)
    goal = order // block_count
    target = jnp.sum(jnp.where(goal[:, None] == shard_ids[None, :], places[None, :], 0), axis=1)
    local_pos = order % block_count
    earlier = (target[None, :] == target[:, None]) & (block_ids[None, :] < block_ids[:, None])
    slot_pos = target * capacity + jnp.sum(earlier.astype(jnp.int32), axis=1)
    slot_ids = jnp.arange(shards * capacity, dtype=jnp.int32)
    matches = slot_ids[:, None] == slot_pos[None, :]
    source_ids = jnp.sum(jnp.where(matches, block_ids[None, :], 0), axis=1)
    outgoing_pos = jnp.sum(jnp.where(matches, local_pos[None, :] + 1, 0), axis=1) - 1
    told = jnp.concatenate(
        [outgoing_pos.reshape(shards, capacity), jnp.broadcast_to(offsets[None, :], (shards, patch_count))], axis=1
    )
    heard = lax.all_to_all(told, "seq", split_axis=0, concat_axis=0, tiled=True)
    blocks = points.reshape(block_count, block_rows, features)
    outgoing = moved_blocks(blocks, source_ids, "send_order")
    arrived = lax.all_to_all(outgoing, "seq", split_axis=0, concat_axis=0, tiled=True)

    arrived_pos = heard[:, :capacity].reshape(-1)
    my_range = jnp.sum(jnp.where(places == lax.axis_index("seq"), shard_ids, 0))
    my_offsets = jnp.sum(jnp.where(shard_ids[:, None] == my_range, heard[:, capacity:], 0), axis=0)
    picked = jnp.sum(jnp.where(arrived_pos[None, :] == block_ids[:, None], slot_ids[None, :], 0), axis=1)
    where = jnp.arange(patch_count, dtype=jnp.int32) + my_offsets + REACH
    half = patch_count // 2

    low, high = normed_patches(arrived, picked, norm_gain, patch_count)
    left = lax.ppermute(high, "seq", ring_next)
    right = lax.ppermute(low, "seq", ring_before)
    wk = w_qkv[:, features : 2 * features]
    wqv = jnp.concatenate([w_qkv[:, :features], w_qkv[:, 2 * features :]], axis=1).T
    query, total, mass, top = own_attention(low, high, wk, wqv, patch_count)
    returning = partner_attention(
        picked,
        where // half,
        where % half,
        (left, low, high, right),
        query,
        total,
        mass,
        top,
        wk,
        wqv[features:],
        w_out,
        arrived,
    )
    homeward = lax.all_to_all(returning, "seq", split_axis=0, concat_axis=0, tiled=True)
    return moved_blocks(homeward, slot_pos, "home_order").reshape(-1, features)


def solution(mesh):
    return jax.shard_map(
        body,
        mesh=mesh,
        in_specs=(
            P(("scene", "seq"), None),
            P(("scene", "seq")),
            P(("scene", "seq")),
            P(),
            P(),
            P(),
        ),
        out_specs=P(("scene", "seq"), None),
        check_vma=False,
    )
```

```python
import functools
import math

import jax
import jax.numpy as jnp
from jax import lax
from jax.experimental import pallas as pl
from jax.experimental.pallas import tpu as pltpu
from jax.sharding import PartitionSpec as P

HEADS = 8
REACH = 2
KEY_TILE = 512
QUERY_TILE = 128
ONES_ROWS = 16
QUARTERS = 8
FIRST = 3
LEAST_MASS = 1e-20
MOST_MASS = 1e30
VMEM_BYTES = 60 * 1024 * 1024
BF = jnp.bfloat16
F32 = jnp.float32


def ring_order(count):
    grids = {16: (4, 2, 2), 64: (4, 4, 4)}
    if count not in grids:
        return list(range(count))
    deep, tall, wide = grids[count]
    columns = [(0, x) for x in range(wide)]
    for y in range(1, tall):
        across = range(wide - 1, 0, -1) if y % 2 else range(1, wide)
        columns += [(y, x) for x in across]
    columns += [(y, 0) for y in range(tall - 1, 0, -1)]
    ring = []
    for at, (y, x) in enumerate(columns):
        along = range(deep) if at % 2 == 0 else range(deep - 1, -1, -1)
        ring += [(z * tall + y) * wide + x for z in along]
    return ring


def params(**more):
    return pltpu.CompilerParams(vmem_limit_bytes=VMEM_BYTES, **more)


def each(count, act):
    def step(i, carry):
        act(i)
        return carry

    lax.fori_loop(0, count, step, 0)


def send_kernel(
    order_ref, offsets_ref, places_ref, points_ref, gain_ref, out_ref, slot_ref, told_ref, points_s, normed_s, taken_s, in_sems, out_sems
):
    block_count, length, features = points_s.shape
    shards = places_ref.shape[0]
    capacity = out_ref.shape[0] // shards
    group = 4

    def copy_in(g):
        rows = pl.ds(g * group, group)
        return pltpu.make_async_copy(points_ref.at[rows], points_s.at[rows], in_sems.at[g])

    def copy_out(b):
        return pltpu.make_async_copy(normed_s.at[b], out_ref.at[slot_ref[b]], out_sems.at[b])

    each(block_count // group, lambda g: copy_in(g).start())

    def clear(d):
        taken_s[d] = 0
        for i in range(capacity):
            told_ref[d * capacity + i] = -1

    each(shards, clear)
    for i in range(offsets_ref.shape[0]):
        told_ref[shards * capacity + i] = offsets_ref[i]

    def place(b):
        position = order_ref[b]
        device = places_ref[lax.div(position, block_count)]
        rank = taken_s[device]
        taken_s[device] = rank + 1
        slot_ref[b] = device * capacity + rank
        told_ref[device * capacity + rank] = lax.rem(position, block_count)

    each(block_count, place)

    def normalise(g):
        copy_in(g).wait()
        values = points_s[pl.ds(g * group, group)].astype(F32).reshape(group * length, features)
        centred = values - jnp.mean(values, axis=-1, keepdims=True)
        spread = jnp.mean(jnp.square(centred), axis=-1, keepdims=True)
        result = (centred * lax.rsqrt(spread + 1e-05) * gain_ref[...]).astype(BF)
        normed_s[pl.ds(g * group, group)] = result.reshape(group, length, features)
        for i in range(group):
            copy_out(g * group + i).start()

    each(block_count // group, normalise)
    each(block_count, lambda b: copy_out(b).wait())


def normed_to_send(blocks, order, offsets, norm_gain, ring, capacity):
    block_count, length, features = blocks.shape
    shards = len(ring)
    return pl.pallas_call(
        send_kernel,
        grid_spec=pltpu.PrefetchScalarGridSpec(
            num_scalar_prefetch=3,
            grid=(1,),
            in_specs=[pl.BlockSpec(memory_space=pl.ANY), pl.BlockSpec((1, features), lambda p, *s: (0, 0))],
            out_specs=[pl.BlockSpec(memory_space=pl.ANY)] + [pl.BlockSpec(memory_space=pltpu.SMEM)] * 2,
            scratch_shapes=[
                pltpu.VMEM(blocks.shape, BF),
                pltpu.VMEM(blocks.shape, BF),
                pltpu.SMEM((shards,), jnp.int32),
                pltpu.SemaphoreType.DMA((block_count // 4,)),
                pltpu.SemaphoreType.DMA((block_count,)),
            ],
        ),
        out_shape=[
            jax.ShapeDtypeStruct((shards * capacity, length, features), BF),
            jax.ShapeDtypeStruct((block_count,), jnp.int32),
            jax.ShapeDtypeStruct((shards * capacity + offsets.shape[0],), jnp.int32),
        ],
        compiler_params=params(),
        name="send",
    )(order, offsets, jnp.asarray(ring, jnp.int32), blocks, norm_gain.reshape(1, features))


def sort_kernel(
    known_ref, here_ref, arrived_ref, low_ref, high_ref, picked_ref, set_ref, within_ref, held_s, in_sems, out_sems
):
    patch_count, _, per_patch = held_s.shape[:3]
    half = patch_count // 2
    slot_count = arrived_ref.shape[0]
    entry = slot_count + patch_count
    capacity = slot_count // (known_ref.shape[0] // entry)
    my_place, my_range = here_ref[0], here_ref[1]

    def copy_in(patch, i):
        at = patch * per_patch + i
        return pltpu.make_async_copy(arrived_ref.at[picked_ref[at]], held_s.at[patch, :, i], in_sems.at[at])

    def copy_out(patch):
        out_ref = low_ref if patch < half else high_ref
        return pltpu.make_async_copy(held_s.at[patch], out_ref.at[patch % half], out_sems.at[patch])

    each(patch_count * per_patch, lambda i: picked_ref.__setitem__(i, 0))

    def find(sender):
        for rank in range(capacity):
            position = known_ref[sender * entry + my_place * capacity + rank]

            @pl.when(position >= 0)
            def _():
                picked_ref[position] = sender * capacity + rank

    each(slot_count // capacity, find)
    for patch in range(patch_count):
        for i in range(per_patch):
            copy_in(patch, i).start()
    for patch in range(patch_count):
        wanted = patch + known_ref[my_range * entry + slot_count + patch] + REACH
        set_ref[patch] = lax.div(wanted, half)
        within_ref[patch] = lax.rem(wanted, half)
    for patch in range(patch_count):
        for i in range(per_patch):
            copy_in(patch, i).wait()
        copy_out(patch).start()
    for patch in range(patch_count):
        copy_out(patch).wait()


def sorted_patches(arrived, known, here, block_count, patch_count):
    _, quarters, length, features = arrived.shape
    per_patch = block_count // patch_count
    half = patch_count // 2
    patch_shape = (quarters, per_patch, length, features)
    counts = (block_count, patch_count, patch_count)
    low, high, *found = pl.pallas_call(
        sort_kernel,
        grid_spec=pltpu.PrefetchScalarGridSpec(
            num_scalar_prefetch=2,
            grid=(1,),
            in_specs=[pl.BlockSpec(memory_space=pl.ANY)],
            out_specs=[pl.BlockSpec(memory_space=pl.ANY)] * 2 + [pl.BlockSpec(memory_space=pltpu.SMEM)] * 3,
            scratch_shapes=[
                pltpu.VMEM((patch_count,) + patch_shape, BF),
                pltpu.SemaphoreType.DMA((block_count,)),
                pltpu.SemaphoreType.DMA((patch_count,)),
            ],
        ),
        out_shape=[jax.ShapeDtypeStruct((half,) + patch_shape, BF)] * 2
        + [jax.ShapeDtypeStruct((count,), jnp.int32) for count in counts],
        compiler_params=params(),
        name="sort",
    )(known, here, arrived)
    return low.reshape(-1, features), high.reshape(-1, features), *found


def home_kernel(slot_ref, points_ref, first_ref, rest_ref, out_ref, points_s, first_s, rest_s, out_s, in_sems, out_sems):
    block_count = points_s.shape[0]
    group = block_count // out_sems.shape[0]

    def copies_in(g):
        rows = pl.ds(g * group, group)
        sems = in_sems.at[g]
        yield pltpu.make_async_copy(points_ref.at[rows], points_s.at[rows], sems.at[0])
        for i in range(group):
            b = g * group + i
            yield pltpu.make_async_copy(first_ref.at[slot_ref[b]], first_s.at[b], sems.at[1 + i])
            yield pltpu.make_async_copy(rest_ref.at[slot_ref[b]], rest_s.at[b], sems.at[1 + group + i])

    def copy_out(g):
        rows = pl.ds(g * group, group)
        return pltpu.make_async_copy(out_s.at[rows], out_ref.at[rows], out_sems.at[g])

    def begin(g):
        for copy in copies_in(g):
            copy.start()

    def add(g):
        for copy in copies_in(g):
            copy.wait()
        rows = pl.ds(g * group, group)
        out_s[rows, :FIRST] = (points_s[rows, :FIRST].astype(F32) + first_s[rows].astype(F32)).astype(BF)
        out_s[rows, FIRST:] = (points_s[rows, FIRST:].astype(F32) + rest_s[rows].astype(F32)).astype(BF)
        copy_out(g).start()

    each(block_count // group, begin)
    each(block_count // group, add)
    each(block_count // group, lambda g: copy_out(g).wait())


def home_sum(blocks, first, rest, slots):
    block_count = blocks.shape[0]
    group = 4
    return pl.pallas_call(
        home_kernel,
        grid_spec=pltpu.PrefetchScalarGridSpec(
            num_scalar_prefetch=1,
            grid=(1,),
            in_specs=[pl.BlockSpec(memory_space=pl.ANY)] * 3,
            out_specs=pl.BlockSpec(memory_space=pl.ANY),
            scratch_shapes=[
                pltpu.VMEM(blocks.shape, BF),
                pltpu.VMEM((block_count,) + first.shape[1:], BF),
                pltpu.VMEM((block_count,) + rest.shape[1:], BF),
                pltpu.VMEM(blocks.shape, BF),
                pltpu.SemaphoreType.DMA((block_count // group, 1 + 2 * group)),
                pltpu.SemaphoreType.DMA((block_count // group,)),
            ],
        ),
        out_shape=jax.ShapeDtypeStruct(blocks.shape, BF),
        compiler_params=params(),
        name="home",
    )(slots, blocks, first, rest)


def nt_dot(a, b):
    return lax.dot_general(a, b, (((1,), (1,)), ((), ())), preferred_element_type=F32)


def in_range(mass):
    good = jnp.logical_and(mass >= LEAST_MASS, mass <= MOST_MASS)
    return jnp.min(jnp.where(good, 1.0, 0.0)) > 0.5


def lone_head(pair, which, width):
    kept = pair[which * width : (which + 1) * width]
    blank = jnp.zeros_like(kept)
    return jnp.concatenate([kept, blank] if which == 0 else [blank, kept], axis=0)


def with_ones(values):
    return jnp.concatenate([values, jnp.ones((ONES_ROWS, values.shape[1]), BF)], axis=0)


def plain_head(query_ref, key_ref, value_ref, head, width):
    pair = 2 * width * (head // 2)
    query = lone_head(query_ref[pair : pair + 2 * width, :], head % 2, width)
    total = None
    for at in range(0, key_ref.shape[0], KEY_TILE):
        scores = jnp.dot(key_ref[at : at + KEY_TILE, pair : pair + 2 * width], query, preferred_element_type=F32)
        raised = jnp.exp(scores).astype(BF)
        values = with_ones(value_ref[head * width : (head + 1) * width, at : at + KEY_TILE])
        part = jnp.dot(values, raised, preferred_element_type=F32)
        total = part if total is None else total + part
    return total


def shifted_heads(query_ref, key_ref, value_ref, width, use):
    tiles = query_ref.shape[1] // QUERY_TILE

    def one(tile):
        columns = pl.ds(pl.multiple_of(tile * QUERY_TILE, QUERY_TILE), QUERY_TILE)
        for head in range(key_ref.shape[1] // width):
            pair = 2 * width * (head // 2)
            features = slice(pair, pair + 2 * width)
            query = lone_head(query_ref[features, columns], head % 2, width)
            scores = jnp.dot(key_ref[:, features], query, preferred_element_type=F32)
            top = jnp.max(scores, axis=0, keepdims=True)
            raised = jnp.exp(scores - top).astype(BF)
            rows = slice(head * width, (head + 1) * width)
            sums = jnp.dot(with_ones(value_ref[rows, :]), raised, preferred_element_type=F32)
            use(rows, head, columns, top, sums)

    each(tiles, one)


def parts_of(columns):
    first = columns * FIRST // QUARTERS
    return (slice(0, first), slice(first, columns))


def own_kernel(low_ref, high_ref, wk_ref, wqv_ref, *refs, width):
    *out_refs, query_s, key_s, value_s, total_s, mass_s, top_s = refs
    patch = pl.program_id(0)
    half = pl.num_programs(0) // 2
    features = wk_ref.shape[0]
    parts = [(columns, out_refs[4 * i : 4 * i + 4]) for i, columns in enumerate(parts_of(query_s.shape[1]))]

    def project(normed_ref):
        normed = normed_ref[...]
        key_s[...] = jnp.dot(normed, wk_ref[...], preferred_element_type=F32).astype(BF)
        both = nt_dot(wqv_ref[...], normed)
        query_s[...] = both[:features].astype(BF) * (1 / math.sqrt(width))
        value_s[...] = both[features:].astype(BF)

    @pl.when(patch < half)
    def _():
        project(low_ref)

    @pl.when(patch >= half)
    def _():
        project(high_ref)

    for columns, (query_ref, _, _, _) in parts:
        query_ref[...] = query_s[:, columns]
    masses = []
    for head in range(features // width):
        sums = plain_head(query_s, key_s, value_s, head, width)
        masses.append(sums[width : width + 1])
        for columns, (_, total_ref, mass_ref, _) in parts:
            total_ref[head * width : (head + 1) * width, :] = sums[:width, columns]
            mass_ref[head : head + 1, :] = sums[width : width + 1, columns]
    for _, (_, _, _, top_ref) in parts:
        top_ref[...] = jnp.zeros_like(top_ref)
    small = in_range(jnp.concatenate(masses, axis=0))

    @pl.when(jnp.logical_not(small))
    def _():
        def use(rows, head, columns, top, sums):
            total_s[rows, columns] = sums[:width]
            mass_s[slice(head, head + 1), columns] = sums[width : width + 1]
            top_s[slice(head, head + 1), columns] = top

        shifted_heads(query_s, key_s, value_s, width, use)
        for columns, (_, total_ref, mass_ref, top_ref) in parts:
            total_ref[...] = total_s[:, columns]
            mass_ref[...] = mass_s[:, columns]
            top_ref[...] = top_s[:, columns]


def own_attention(low, high, wk, wqv, patch_count):
    features = wk.shape[0]
    half = patch_count // 2
    rows = low.shape[0] // half
    width = features // HEADS
    whole = lambda p: (0, 0)
    along = lambda p: (0, p)
    specs, shapes = [], []
    for columns in parts_of(rows):
        count = columns.stop - columns.start
        for height, dtype in ((features, BF), (features, F32), (HEADS, F32), (HEADS, F32)):
            specs.append(pl.BlockSpec((height, count), along))
            shapes.append(jax.ShapeDtypeStruct((height, patch_count * count), dtype))
    results = pl.pallas_call(
        functools.partial(own_kernel, width=width),
        grid=(patch_count,),
        in_specs=[
            pl.BlockSpec((rows, features), lambda p: (jnp.minimum(p, half - 1), 0)),
            pl.BlockSpec((rows, features), lambda p: (jnp.maximum(p - half, 0), 0)),
            pl.BlockSpec(wk.shape, whole),
            pl.BlockSpec(wqv.shape, whole),
        ],
        out_specs=specs,
        out_shape=shapes,
        scratch_shapes=[
            pltpu.VMEM((features, rows), BF),
            pltpu.VMEM((rows, features), BF),
            pltpu.VMEM((features, rows), BF),
            pltpu.VMEM((features, rows), F32),
            pltpu.VMEM((HEADS, rows), F32),
            pltpu.VMEM((HEADS, rows), F32),
        ],
        compiler_params=params(),
        cost_estimate=pl.CostEstimate(flops=40 * 10**9, bytes_accessed=28 * 10**6, transcendentals=0),
        name="own",
    )(low, high, wk, wqv)
    return results[:4], results[4:]


def attend_partner(picked_ref, query_ref, total_ref, mass_ref, top_ref, key_ref, value_ref, wo_ref, out_ref, mixed_s):
    patch = pl.program_id(0)
    width = wo_ref.shape[0] // HEADS
    _, quarters, length, _ = out_ref.shape
    per_patch = mixed_s.shape[1] // (quarters * length)

    def finish():
        mixed = lax.dot_general(mixed_s[...], wo_ref[...], (((0,), (0,)), ((), ())), preferred_element_type=F32)
        mixed = mixed.astype(BF)
        for i in range(per_patch):
            slot = picked_ref[patch * per_patch + i]
            for quarter in range(quarters):
                at = (quarter * per_patch + i) * length
                out_ref[slot, quarter] = mixed[at : at + length]

    masses = []
    for head in range(HEADS):
        sums = plain_head(query_ref, key_ref, value_ref, head, width)
        rows = slice(head * width, (head + 1) * width)
        masses.append(mass_ref[head : head + 1, :] + sums[width : width + 1])
        mixed_s[rows, :] = ((total_ref[rows, :] + sums[:width]) * (1.0 / masses[-1])).astype(BF)
    unshifted = jnp.max(jnp.abs(top_ref[...])) == 0.0
    small = jnp.logical_and(in_range(jnp.concatenate(masses, axis=0)), unshifted)
    finish()

    @pl.when(jnp.logical_not(small))
    def _():
        def use(rows, head, columns, top, sums):
            one = slice(head, head + 1)
            before = top_ref[one, columns]
            highest = jnp.maximum(before, top)
            mine, theirs = jnp.exp(before - highest), jnp.exp(top - highest)
            mass = mass_ref[one, columns] * mine + sums[width : width + 1] * theirs
            mixed_s[rows, columns] = ((total_ref[rows, columns] * mine + sums[:width] * theirs) / mass).astype(BF)

        shifted_heads(query_ref, key_ref, value_ref, width, use)
        finish()


def first_kernel(picked_ref, source_ref, within_ref, left_ref, low_ref, high_ref, right_ref, *refs):
    *between, wk_ref, wv_ref, wo_ref, out_ref, key_ref, value_ref, normed_s, mixed_s, sems = refs
    patch = pl.program_id(0)
    rows = normed_s.shape[1]
    now = lax.rem(patch, 2)

    def copy(number, which, at):
        return pltpu.make_async_copy(number.at[pl.ds(which * rows, rows)], normed_s.at[at], sems.at[at])

    def begin(which):
        for number, normed_ref in enumerate((left_ref, low_ref, high_ref, right_ref)):

            @pl.when(source_ref[which] == number)
            def _(normed_ref=normed_ref):
                copy(normed_ref, within_ref[which], lax.rem(which, 2)).start()

    @pl.when(patch == 0)
    def _():
        begin(patch)

    @pl.when(patch + 1 < pl.num_programs(0))
    def _():
        begin(patch + 1)

    copy(low_ref, 0, now).wait()
    normed = normed_s[now]
    key_ref[...] = jnp.dot(normed, wk_ref[...], preferred_element_type=F32).astype(BF)
    value_ref[...] = nt_dot(wv_ref[...], normed).astype(BF)
    attend_partner(picked_ref, *between, key_ref, value_ref, wo_ref, out_ref, mixed_s)


def rest_kernel(picked_ref, *refs):
    attend_partner(picked_ref, *refs)


def own_specs(own, patch_count):
    return [pl.BlockSpec((part.shape[0], part.shape[1] // patch_count), lambda p, *s: (0, p)) for part in own]


def partner_first(picked, source, within, sets, own, wk, wqv, wo, out_shape):
    features = wk.shape[0]
    patch_count = source.shape[0]
    rows = sets[0].shape[0] // (patch_count // 2)
    whole = lambda p, *s: (0, 0)
    below = lambda p, *s: (1, 0)

    return pl.pallas_call(
        first_kernel,
        grid_spec=pltpu.PrefetchScalarGridSpec(
            num_scalar_prefetch=3,
            grid=(patch_count,),
            in_specs=[pl.BlockSpec(memory_space=pl.ANY)] * 4
            + own_specs(own, patch_count)
            + [pl.BlockSpec(wk.shape, whole), pl.BlockSpec(wk.shape, below), pl.BlockSpec(wo.shape, whole)],
            out_specs=[
                pl.BlockSpec(out_shape, lambda p, *s: (0, 0, 0, 0)),
                pl.BlockSpec((rows, features), lambda p, *s: (p, 0)),
                pl.BlockSpec((features, rows), lambda p, *s: (0, p)),
            ],
            scratch_shapes=[
                pltpu.VMEM((2, rows, features), BF),
                pltpu.VMEM((features, own[0].shape[1] // patch_count), BF),
                pltpu.SemaphoreType.DMA((2,)),
            ],
        ),
        out_shape=[
            jax.ShapeDtypeStruct(out_shape, BF),
            jax.ShapeDtypeStruct((patch_count * rows, features), BF),
            jax.ShapeDtypeStruct((features, patch_count * rows), BF),
        ],
        compiler_params=params(),
        cost_estimate=pl.CostEstimate(flops=15 * 10**9, bytes_accessed=28 * 10**6, transcendentals=0),
        name="partner_first",
    )(picked, source, within, *sets, *own, wk, wqv, wo)


def partner_rest(picked, own, keys, values, wo, out_shape, patch_count):
    features = wo.shape[0]
    rows = keys.shape[0] // patch_count
    return pl.pallas_call(
        rest_kernel,
        grid_spec=pltpu.PrefetchScalarGridSpec(
            num_scalar_prefetch=1,
            grid=(patch_count,),
            in_specs=own_specs(own, patch_count)
            + [
                pl.BlockSpec((rows, features), lambda p, *s: (p, 0)),
                pl.BlockSpec((features, rows), lambda p, *s: (0, p)),
                pl.BlockSpec(wo.shape, lambda p, *s: (0, 0)),
            ],
            out_specs=pl.BlockSpec(out_shape, lambda p, *s: (0, 0, 0, 0)),
            scratch_shapes=[pltpu.VMEM((features, own[0].shape[1] // patch_count), BF)],
        ),
        out_shape=jax.ShapeDtypeStruct(out_shape, BF),
        compiler_params=params(),
        cost_estimate=pl.CostEstimate(flops=30 * 10**9, bytes_accessed=28 * 10**6, transcendentals=0),
        name="partner_rest",
    )(picked, *own, keys, values, wo)


def exchanged(value):
    return lax.all_to_all(value, "seq", split_axis=0, concat_axis=0, tiled=True)


def body(points, order, offsets, norm_gain, w_qkv, w_out):
    features = points.shape[1]
    block_count = order.shape[0]
    block_rows = points.shape[0] // block_count
    patch_count = offsets.shape[0]
    shards = lax.axis_size("seq")
    capacity = (block_count + shards - 1) // shards
    ring = ring_order(shards)
    ring_next = [(ring[e], ring[(e + 1) % shards]) for e in range(shards)]
    ring_before = [(ring[e], ring[e - 1]) for e in range(shards)]
    me = lax.axis_index("seq")
    ranges = [ring.index(place) for place in range(shards)]
    here = lax.dynamic_slice(jnp.asarray(list(enumerate(ranges)), jnp.int32), (me, 0), (1, 2)).reshape(2)

    blocks = points.reshape(block_count, block_rows, features)
    outgoing, slots, told = normed_to_send(blocks, order, offsets, norm_gain, ring, capacity)
    arrived = exchanged(outgoing).reshape(-1, QUARTERS, block_rows // QUARTERS, features)
    known = lax.all_gather(told, "seq", tiled=True)
    low, high, picked, source, within = sorted_patches(arrived, known, here, block_count, patch_count)
    left = lax.ppermute(high, "seq", ring_next)
    right = lax.ppermute(low, "seq", ring_before)
    wk = w_qkv[:, features : 2 * features]
    wqv = jnp.concatenate([w_qkv[:, :features], w_qkv[:, 2 * features :]], axis=1).T
    own_first, own_rest = own_attention(low, high, wk, wqv, patch_count)
    slot_shape = arrived.shape[:1], arrived.shape[2:]
    first, keys, values = partner_first(
        picked,
        source,
        within,
        (left, low, high, right),
        own_first,
        wk,
        wqv,
        w_out,
        slot_shape[0] + (FIRST,) + slot_shape[1],
    )
    first_home = exchanged(first)
    rest = partner_rest(
        picked, own_rest, keys, values, w_out, slot_shape[0] + (QUARTERS - FIRST,) + slot_shape[1], patch_count
    )
    rest_home = exchanged(rest)
    split_blocks = blocks.reshape(block_count, QUARTERS, block_rows // QUARTERS, features)
    return home_sum(split_blocks, first_home, rest_home, slots).reshape(-1, features)


def solution(mesh):
    return jax.shard_map(
        body,
        mesh=mesh,
        in_specs=(
            P(("scene", "seq"), None),
            P(("scene", "seq")),
            P(("scene", "seq")),
            P(),
            P(),
            P(),
        ),
        out_specs=P(("scene", "seq"), None),
        check_vma=False,
    )
```

```python
import functools
import math

import jax
import jax.numpy as jnp
from jax import lax
from jax.experimental import pallas as pl
from jax.experimental.pallas import tpu as pltpu
from jax.sharding import PartitionSpec as P

HEADS = 8
REACH = 2
KEY_TILE = 1024
QUERY_TILE = 128
ONES_ROWS = 16
QUARTERS = 4
FIRST = 2
LEAST_MASS = 1e-20
MOST_MASS = 1e30
VMEM_BYTES = 62 * 1024 * 1024
BF = jnp.bfloat16
F32 = jnp.float32


def ring_order(count):
    grids = {16: (4, 2, 2), 64: (4, 4, 4)}
    if count not in grids:
        return list(range(count))
    deep, tall, wide = grids[count]
    columns = [(0, x) for x in range(wide)]
    for y in range(1, tall):
        across = range(wide - 1, 0, -1) if y % 2 else range(1, wide)
        columns += [(y, x) for x in across]
    columns += [(y, 0) for y in range(tall - 1, 0, -1)]
    ring = []
    for at, (y, x) in enumerate(columns):
        along = range(deep) if at % 2 == 0 else range(deep - 1, -1, -1)
        ring += [(z * tall + y) * wide + x for z in along]
    return ring


def params(**more):
    return pltpu.CompilerParams(vmem_limit_bytes=VMEM_BYTES, **more)


def each(count, act):
    def step(i, carry):
        act(i)
        return carry

    lax.fori_loop(0, count, step, 0)


def send_kernel(
    order_ref, offsets_ref, places_ref, points_ref, gain_ref, out_ref, slot_ref, told_ref, points_s, normed_s, taken_s, in_sems, out_sems
):
    block_count, length, features = points_s.shape
    shards = places_ref.shape[0]
    capacity = out_ref.shape[0] // shards
    group = 4

    def copy_in(g):
        rows = pl.ds(g * group, group)
        return pltpu.make_async_copy(points_ref.at[rows], points_s.at[rows], in_sems.at[g])

    def copy_out(b):
        return pltpu.make_async_copy(normed_s.at[b], out_ref.at[slot_ref[b]], out_sems.at[b])

    each(block_count // group, lambda g: copy_in(g).start())

    def clear(d):
        taken_s[d] = 0
        for i in range(capacity):
            told_ref[d * capacity + i] = -1

    each(shards, clear)
    for i in range(offsets_ref.shape[0]):
        told_ref[shards * capacity + i] = offsets_ref[i]

    def place(b):
        position = order_ref[b]
        device = places_ref[lax.div(position, block_count)]
        rank = taken_s[device]
        taken_s[device] = rank + 1
        slot_ref[b] = device * capacity + rank
        told_ref[device * capacity + rank] = lax.rem(position, block_count)

    each(block_count, place)

    def normalise(g):
        copy_in(g).wait()
        values = points_s[pl.ds(g * group, group)].astype(F32).reshape(group * length, features)
        centred = values - jnp.mean(values, axis=-1, keepdims=True)
        spread = jnp.mean(jnp.square(centred), axis=-1, keepdims=True)
        result = (centred * lax.rsqrt(spread + 1e-05) * gain_ref[...]).astype(BF)
        normed_s[pl.ds(g * group, group)] = result.reshape(group, length, features)
        for i in range(group):
            copy_out(g * group + i).start()

    each(block_count // group, normalise)
    each(block_count, lambda b: copy_out(b).wait())


def normed_to_send(blocks, order, offsets, norm_gain, ring, capacity):
    block_count, length, features = blocks.shape
    shards = len(ring)
    return pl.pallas_call(
        send_kernel,
        grid_spec=pltpu.PrefetchScalarGridSpec(
            num_scalar_prefetch=3,
            grid=(1,),
            in_specs=[pl.BlockSpec(memory_space=pl.ANY), pl.BlockSpec((1, features), lambda p, *s: (0, 0))],
            out_specs=[pl.BlockSpec(memory_space=pl.ANY)] + [pl.BlockSpec(memory_space=pltpu.SMEM)] * 2,
            scratch_shapes=[
                pltpu.VMEM(blocks.shape, BF),
                pltpu.VMEM(blocks.shape, BF),
                pltpu.SMEM((shards,), jnp.int32),
                pltpu.SemaphoreType.DMA((block_count // 4,)),
                pltpu.SemaphoreType.DMA((block_count,)),
            ],
        ),
        out_shape=[
            jax.ShapeDtypeStruct((shards * capacity, length, features), BF),
            jax.ShapeDtypeStruct((block_count,), jnp.int32),
            jax.ShapeDtypeStruct((shards * capacity + offsets.shape[0],), jnp.int32),
        ],
        compiler_params=params(),
        name="send",
    )(order, offsets, jnp.asarray(ring, jnp.int32), blocks, norm_gain.reshape(1, features))


def sort_kernel(known_ref, ranges_ref, arrived_ref, *refs):
    *out_refs, picked_ref, set_ref, within_ref, held_s, in_sems, out_sems = refs
    patch_count, _, per_patch = held_s.shape[:3]
    half = patch_count // 2
    slot_count = arrived_ref.shape[0]
    entry = slot_count + patch_count
    capacity = slot_count // (known_ref.shape[0] // entry)
    my_place = lax.axis_index("seq")
    my_range = ranges_ref[my_place]

    def copy_in(patch, i):
        at = patch * per_patch + i
        return pltpu.make_async_copy(arrived_ref.at[picked_ref[at]], held_s.at[patch, :, i], in_sems.at[at])

    def copies_out(patch):
        for chunk, quarters in enumerate((slice(0, FIRST), slice(FIRST, QUARTERS))):
            count = quarters.stop - quarters.start
            out_ref = out_refs[2 * chunk + patch // half]
            yield pltpu.make_async_copy(
                held_s.at[patch, pl.ds(quarters.start, count)], out_ref.at[patch % half], out_sems.at[patch, chunk]
            )

    each(patch_count * per_patch, lambda i: picked_ref.__setitem__(i, 0))

    def find(sender):
        for rank in range(capacity):
            position = known_ref[sender * entry + my_place * capacity + rank]

            @pl.when(position >= 0)
            def _():
                picked_ref[position] = sender * capacity + rank

    each(slot_count // capacity, find)
    for patch in range(patch_count):
        for i in range(per_patch):
            copy_in(patch, i).start()
    for patch in range(patch_count):
        wanted = patch + known_ref[my_range * entry + slot_count + patch] + REACH
        set_ref[patch] = lax.div(wanted, half)
        within_ref[patch] = lax.rem(wanted, half)
    for patch in range(patch_count):
        for i in range(per_patch):
            copy_in(patch, i).wait()
        for copy in copies_out(patch):
            copy.start()
    for patch in range(patch_count):
        for copy in copies_out(patch):
            copy.wait()


def sorted_patches(arrived, known, ranges, block_count, patch_count):
    _, quarters, length, features = arrived.shape
    per_patch = block_count // patch_count
    half = patch_count // 2
    patch_shape = (quarters, per_patch, length, features)
    counts = (block_count, patch_count, patch_count)
    chunk_shapes = [(half, count, per_patch, length, features) for count in (FIRST, quarters - FIRST) for _ in range(2)]
    results = pl.pallas_call(
        sort_kernel,
        grid_spec=pltpu.PrefetchScalarGridSpec(
            num_scalar_prefetch=2,
            grid=(1,),
            in_specs=[pl.BlockSpec(memory_space=pl.ANY)],
            out_specs=[pl.BlockSpec(memory_space=pl.ANY)] * 4 + [pl.BlockSpec(memory_space=pltpu.SMEM)] * 3,
            scratch_shapes=[
                pltpu.VMEM((patch_count,) + patch_shape, BF),
                pltpu.SemaphoreType.DMA((block_count,)),
                pltpu.SemaphoreType.DMA((patch_count, 2)),
            ],
        ),
        out_shape=[jax.ShapeDtypeStruct(shape, BF) for shape in chunk_shapes]
        + [jax.ShapeDtypeStruct((count,), jnp.int32) for count in counts],
        compiler_params=params(),
        name="sort",
    )(known, jnp.asarray(ranges, jnp.int32), arrived)
    return [chunk.reshape(-1, features) for chunk in results[:4]], results[4:]


def home_kernel(slot_ref, points_ref, part_ref, *refs, start):
    out_ref, points_s, part_s, out_s, in_sems, out_sems = refs[-6:]
    block_count, quarters = points_s.shape[:2]
    group = block_count // out_sems.shape[0]

    def place(g):
        return pl.ds(g * group, group), pl.ds(start, quarters)

    def copies_in(g):
        sems = in_sems.at[g]
        yield pltpu.make_async_copy(points_ref.at[place(g)], points_s.at[pl.ds(g * group, group)], sems.at[0])
        for i in range(group):
            b = g * group + i
            yield pltpu.make_async_copy(part_ref.at[slot_ref[b]], part_s.at[b], sems.at[1 + i])

    def copy_out(g):
        return pltpu.make_async_copy(out_s.at[pl.ds(g * group, group)], out_ref.at[place(g)], out_sems.at[g])

    def begin(g):
        for copy in copies_in(g):
            copy.start()

    def add(g):
        for copy in copies_in(g):
            copy.wait()
        rows = pl.ds(g * group, group)
        out_s[rows] = (points_s[rows].astype(F32) + part_s[rows].astype(F32)).astype(BF)
        copy_out(g).start()

    each(block_count // group, begin)
    each(block_count // group, add)
    each(block_count // group, lambda g: copy_out(g).wait())


def home_sum(blocks, part, slots, start, result=None):
    block_count = blocks.shape[0]
    group = 4
    chunk_shape = (block_count,) + part.shape[1:]
    operands = (slots, blocks, part) + (() if result is None else (result,))
    return pl.pallas_call(
        functools.partial(home_kernel, start=start),
        grid_spec=pltpu.PrefetchScalarGridSpec(
            num_scalar_prefetch=1,
            grid=(1,),
            in_specs=[pl.BlockSpec(memory_space=pl.ANY)] * (len(operands) - 1),
            out_specs=pl.BlockSpec(memory_space=pl.ANY),
            scratch_shapes=[
                pltpu.VMEM(chunk_shape, BF),
                pltpu.VMEM(chunk_shape, BF),
                pltpu.VMEM(chunk_shape, BF),
                pltpu.SemaphoreType.DMA((block_count // group, 1 + group)),
                pltpu.SemaphoreType.DMA((block_count // group,)),
            ],
        ),
        out_shape=jax.ShapeDtypeStruct(blocks.shape, BF),
        input_output_aliases={} if result is None else {3: 0},
        compiler_params=params(),
        cost_estimate=cost(5),
        name="home",
    )(*operands)


def nt_dot(a, b):
    return lax.dot_general(a, b, (((1,), (1,)), ((), ())), preferred_element_type=F32)


def in_range(mass):
    good = jnp.logical_and(mass >= LEAST_MASS, mass <= MOST_MASS)
    return jnp.min(jnp.where(good, 1.0, 0.0)) > 0.5


def lone_head(pair, which, width):
    kept = pair[which * width : (which + 1) * width]
    blank = jnp.zeros_like(kept)
    return jnp.concatenate([kept, blank] if which == 0 else [blank, kept], axis=0)


def with_ones(values):
    return jnp.concatenate([values, jnp.ones((ONES_ROWS, values.shape[1]), BF)], axis=0)


def plain_head(query_ref, key_ref, value_ref, head, width):
    pair = 2 * width * (head // 2)
    query = lone_head(query_ref[pair : pair + 2 * width, :], head % 2, width)
    total = None
    for at in range(0, key_ref.shape[0], KEY_TILE):
        scores = jnp.dot(key_ref[at : at + KEY_TILE, pair : pair + 2 * width], query, preferred_element_type=F32)
        raised = jnp.exp(scores).astype(BF)
        values = with_ones(value_ref[head * width : (head + 1) * width, at : at + KEY_TILE])
        part = jnp.dot(values, raised, preferred_element_type=F32)
        total = part if total is None else total + part
    return total


def plain_sums(query_ref, pieces, before, width, emit):
    masses = []
    for head in range(query_ref.shape[0] // width):
        rows, one = slice(head * width, (head + 1) * width), slice(head, head + 1)
        sums = None
        for key_ref, value_ref in pieces:
            part = plain_head(query_ref, key_ref, value_ref, head, width)
            sums = part if sums is None else sums + part
        total, mass = sums[:width], sums[width : width + 1]
        if before is not None:
            total, mass = total + before[0][rows, :], mass + before[1][one, :]
        masses.append(mass)
        emit(rows, one, slice(None), total, mass, jnp.zeros_like(mass))
    good = in_range(jnp.concatenate(masses, axis=0))
    if before is not None:
        good = jnp.logical_and(good, jnp.max(jnp.abs(before[2][...])) == 0.0)
    return good


def shifted_sums(query_ref, pieces, before, width, emit):
    def step(tile):
        columns = pl.ds(pl.multiple_of(tile * QUERY_TILE, QUERY_TILE), QUERY_TILE)
        for head in range(query_ref.shape[0] // width):
            rows, one = slice(head * width, (head + 1) * width), slice(head, head + 1)
            pair = 2 * width * (head // 2)
            features = slice(pair, pair + 2 * width)
            query = lone_head(query_ref[features, columns], head % 2, width)
            total = mass = top = None
            if before is not None:
                total, mass, top = before[0][rows, columns], before[1][one, columns], before[2][one, columns]
            for key_ref, value_ref in pieces:
                scores = jnp.dot(key_ref[:, features], query, preferred_element_type=F32)
                highest = jnp.max(scores, axis=0, keepdims=True)
                if top is not None:
                    highest = jnp.maximum(highest, top)
                raised = jnp.exp(scores - highest).astype(BF)
                sums = jnp.dot(with_ones(value_ref[rows, :]), raised, preferred_element_type=F32)
                if top is None:
                    total, mass = sums[:width], sums[width : width + 1]
                else:
                    scale = jnp.exp(top - highest)
                    total, mass = total * scale + sums[:width], mass * scale + sums[width : width + 1]
                top = highest
            emit(rows, one, columns, total, mass, top)

    each(query_ref.shape[1] // QUERY_TILE, step)


def attend(query_ref, pieces, before, emit, finish=None):
    width = query_ref.shape[0] // HEADS
    good = plain_sums(query_ref, pieces, before, width, emit)
    if finish is not None:
        finish()

    @pl.when(jnp.logical_not(good))
    def _():
        shifted_sums(query_ref, pieces, before, width, emit)
        if finish is not None:
            finish()


def keep_in(total_ref, mass_ref, top_ref):
    def emit(rows, one, columns, total, mass, top):
        total_ref[rows, columns] = total
        mass_ref[one, columns] = mass
        top_ref[one, columns] = top

    return emit


def normalise_in(mixed_s):
    def emit(rows, one, columns, total, mass, top):
        mixed_s[rows, columns] = (total * (1.0 / mass)).astype(BF)

    return emit


def projected_out(picked_ref, wo_ref, out_ref, mixed_s):
    _, quarters, length, _ = out_ref.shape
    per_patch = mixed_s.shape[1] // (quarters * length)

    def finish():
        mixed = lax.dot_general(mixed_s[...], wo_ref[...], (((0,), (0,)), ((), ())), preferred_element_type=F32)
        mixed = mixed.astype(BF)
        for i in range(per_patch):
            slot = picked_ref[pl.program_id(0) * per_patch + i]
            for quarter in range(quarters):
                at = (quarter * per_patch + i) * length
                out_ref[slot, quarter] = mixed[at : at + length]

    return finish


def own_kernel(low0_ref, high0_ref, low1_ref, high1_ref, wk_ref, wqv_ref, *refs):
    query0_ref, query1_ref, key_ref, value_ref, *state_refs = refs
    patch = pl.program_id(0)
    half = pl.num_programs(0) // 2
    features = wk_ref.shape[0]

    def project(chunks):
        at = 0
        for normed_ref, query_ref in zip(chunks, (query0_ref, query1_ref)):
            normed = normed_ref[...]
            rows = slice(at, at + normed.shape[0])
            key_ref[rows, :] = jnp.dot(normed, wk_ref[...], preferred_element_type=F32).astype(BF)
            both = nt_dot(wqv_ref[...], normed)
            query_ref[...] = both[:features].astype(BF) * math.sqrt(HEADS / features)
            value_ref[:, rows] = both[features:].astype(BF)
            at = rows.stop

    @pl.when(patch < half)
    def _():
        project((low0_ref, low1_ref))

    @pl.when(patch >= half)
    def _():
        project((high0_ref, high1_ref))

    attend(query0_ref, [(key_ref, value_ref)], None, keep_in(*state_refs))


def along(p, *s):
    return (0, p)


def down(p, *s):
    return (p, 0)


def whole(p, *s):
    return (0, 0)


def cost(microseconds):
    return pl.CostEstimate(flops=microseconds * 10**9, bytes_accessed=28 * 10**6, transcendentals=0)


def split_specs(arrays, patch_count):
    return [pl.BlockSpec((part.shape[0], part.shape[1] // patch_count), along) for part in arrays]


def own_attention(chunks, wk, wqv, patch_count):
    features = wk.shape[0]
    half = patch_count // 2
    counts = [chunk.shape[0] // half for chunk in chunks]
    rows = counts[0] + counts[2]
    shapes = [
        jax.ShapeDtypeStruct((features, patch_count * counts[0]), BF),
        jax.ShapeDtypeStruct((features, patch_count * counts[2]), BF),
        jax.ShapeDtypeStruct((patch_count * rows, features), BF),
        jax.ShapeDtypeStruct((features, patch_count * rows), BF),
        jax.ShapeDtypeStruct((features, patch_count * counts[0]), F32),
        jax.ShapeDtypeStruct((HEADS, patch_count * counts[0]), F32),
        jax.ShapeDtypeStruct((HEADS, patch_count * counts[0]), F32),
    ]
    specs = split_specs(shapes, patch_count)
    specs[2] = pl.BlockSpec((rows, features), down)
    lower = lambda p: (jnp.minimum(p, half - 1), 0)
    upper = lambda p: (jnp.maximum(p - half, 0), 0)
    query0, query1, keys, values, *state = pl.pallas_call(
        own_kernel,
        grid=(patch_count,),
        in_specs=[
            pl.BlockSpec((count, features), upper if i % 2 else lower) for i, count in enumerate(counts)
        ]
        + [pl.BlockSpec(wk.shape, whole), pl.BlockSpec(wqv.shape, whole)],
        out_specs=specs,
        out_shape=shapes,
        compiler_params=params(),
        cost_estimate=cost(26),
        name="own",
    )(*chunks, wk, wqv)
    return query0, query1, keys, values, state


def partner_kernel(picked_ref, source_ref, within_ref, *refs, last):
    set_refs, refs = refs[:4], refs[4:]
    query_ref, *before = refs[:4]
    wk_ref, wv_ref = refs[4:6]
    if last:
        wo_ref, out_ref, key_ref, value_ref, normed_s, sems, mixed_s = refs[6:]
    else:
        key_ref, value_ref, *state_refs, normed_s, sems = refs[6:]
    patch = pl.program_id(0)
    rows = normed_s.shape[1]
    now = lax.rem(patch, 2)

    def copy(set_ref, which, at):
        return pltpu.make_async_copy(set_ref.at[pl.ds(which * rows, rows)], normed_s.at[at], sems.at[at])

    def begin(which):
        for number, set_ref in enumerate(set_refs):

            @pl.when(source_ref[which] == number)
            def _(set_ref=set_ref):
                copy(set_ref, within_ref[which], lax.rem(which, 2)).start()

    @pl.when(patch == 0)
    def _():
        begin(patch)

    @pl.when(patch + 1 < pl.num_programs(0))
    def _():
        begin(patch + 1)

    copy(set_refs[1], 0, now).wait()
    normed = normed_s[now]
    key_ref[...] = jnp.dot(normed, wk_ref[...], preferred_element_type=F32).astype(BF)
    value_ref[...] = nt_dot(wv_ref[...], normed).astype(BF)
    pieces = [(key_ref, value_ref)]
    if last:
        attend(query_ref, pieces, before, normalise_in(mixed_s), projected_out(picked_ref, wo_ref, out_ref, mixed_s))
    else:
        attend(query_ref, pieces, before, keep_in(*state_refs))


def partner_chunk(places, sets, query, state, wk, wqv, wo=None, out_shape=None):
    features = wk.shape[0]
    patch_count = places[1].shape[0]
    rows = sets[0].shape[0] // (patch_count // 2)
    last = wo is not None
    held = (query, *state)
    made = [
        jax.ShapeDtypeStruct((patch_count * rows, features), BF),
        jax.ShapeDtypeStruct((features, patch_count * rows), BF),
    ]
    made_specs = [pl.BlockSpec((rows, features), down), pl.BlockSpec((features, rows), along)]
    weights = (wk, wqv) + ((wo,) if last else ())
    weight_specs = [pl.BlockSpec(wk.shape, whole), pl.BlockSpec(wk.shape, lambda p, *s: (1, 0))]
    scratch = [pltpu.VMEM((2, rows, features), BF), pltpu.SemaphoreType.DMA((2,))]
    if last:
        weight_specs.append(pl.BlockSpec(wo.shape, whole))
        made = [jax.ShapeDtypeStruct(out_shape, BF)] + made
        made_specs = [pl.BlockSpec(out_shape, lambda p, *s: (0, 0, 0, 0))] + made_specs
        scratch.append(pltpu.VMEM((features, query.shape[1] // patch_count), BF))
    else:
        made += [jax.ShapeDtypeStruct(part.shape, part.dtype) for part in state]
        made_specs += split_specs(state, patch_count)
    return pl.pallas_call(
        functools.partial(partner_kernel, last=last),
        grid_spec=pltpu.PrefetchScalarGridSpec(
            num_scalar_prefetch=3,
            grid=(patch_count,),
            in_specs=[pl.BlockSpec(memory_space=pl.ANY)] * 4 + split_specs(held, patch_count) + weight_specs,
            out_specs=made_specs,
            scratch_shapes=scratch,
        ),
        out_shape=made,
        compiler_params=params(),
        cost_estimate=cost(15),
        name="partner_last" if last else "partner_next",
    )(*places, *sets, *held, *weights)


def rest_kernel(picked_ref, query_ref, *refs):
    *piece_refs, wo_ref, out_ref, mixed_s = refs
    pieces = list(zip(piece_refs[::2], piece_refs[1::2]))
    attend(query_ref, pieces, None, normalise_in(mixed_s), projected_out(picked_ref, wo_ref, out_ref, mixed_s))


def rest_attention(picked, query, pieces, wo, out_shape, patch_count):
    features = wo.shape[0]
    piece_specs = []
    for keys, _ in pieces:
        rows = keys.shape[0] // patch_count
        piece_specs += [pl.BlockSpec((rows, features), down), pl.BlockSpec((features, rows), along)]
    return pl.pallas_call(
        rest_kernel,
        grid_spec=pltpu.PrefetchScalarGridSpec(
            num_scalar_prefetch=1,
            grid=(patch_count,),
            in_specs=split_specs((query,), patch_count) + piece_specs + [pl.BlockSpec(wo.shape, whole)],
            out_specs=pl.BlockSpec(out_shape, lambda p, *s: (0, 0, 0, 0)),
            scratch_shapes=[pltpu.VMEM((features, query.shape[1] // patch_count), BF)],
        ),
        out_shape=jax.ShapeDtypeStruct(out_shape, BF),
        compiler_params=params(),
        cost_estimate=cost(38),
        name="rest",
    )(picked, query, *[array for piece in pieces for array in piece], wo)


def told_by_all(told):
    shards = lax.axis_size("seq")
    if shards & (shards - 1):
        return lax.all_gather(told, "seq", tiled=True)
    me = lax.axis_index("seq")
    step = 1
    while step < shards:
        other = lax.ppermute(told, "seq", [(place, place ^ step) for place in range(shards)])
        told = jnp.where((me & step) == 0, jnp.concatenate([told, other]), jnp.concatenate([other, told]))
        step *= 2
    return told


def exchanged(value):
    return lax.all_to_all(value, "seq", split_axis=0, concat_axis=0, tiled=True)


def body(points, order, offsets, norm_gain, w_qkv, w_out):
    features = points.shape[1]
    block_count = order.shape[0]
    block_rows = points.shape[0] // block_count
    patch_count = offsets.shape[0]
    shards = lax.axis_size("seq")
    capacity = (block_count + shards - 1) // shards
    ring = ring_order(shards)
    ring_next = [(ring[e], ring[(e + 1) % shards]) for e in range(shards)]
    ring_before = [(ring[e], ring[e - 1]) for e in range(shards)]
    ranges = [ring.index(place) for place in range(shards)]
    wk = w_qkv[:, features : 2 * features]
    wqv = jnp.concatenate([w_qkv[:, :features], w_qkv[:, 2 * features :]], axis=1).T

    blocks = points.reshape(block_count, block_rows, features)
    outgoing, slots, told = normed_to_send(blocks, order, offsets, norm_gain, ring, capacity)
    arrived = exchanged(outgoing).reshape(-1, QUARTERS, block_rows // QUARTERS, features)
    known = told_by_all(told)
    chunks, places = sorted_patches(arrived, known, ranges, block_count, patch_count)
    sets = []
    for low, high in (chunks[:2], chunks[2:]):
        left = lax.ppermute(high, "seq", ring_next)
        right = lax.ppermute(low, "seq", ring_before)
        sets.append((left, low, high, right))
    query0, query1, keys, values, state = own_attention(chunks, wk, wqv, patch_count)
    slot_count, _, length, _ = arrived.shape
    keys0, values0, *state = partner_chunk(places, sets[0], query0, state, wk, wqv)
    first, keys1, values1 = partner_chunk(
        places, sets[1], query0, state, wk, wqv, w_out, (slot_count, FIRST, length, features)
    )
    first_home = exchanged(first)
    pieces = [(keys, values), (keys0, values0), (keys1, values1)]
    rest = rest_attention(
        places[0], query1, pieces, w_out, (slot_count, QUARTERS - FIRST, length, features), patch_count
    )
    rest, first_home = lax.optimization_barrier((rest, first_home))
    rest_home = exchanged(rest)
    split_blocks = blocks.reshape(block_count, QUARTERS, block_rows // QUARTERS, features)
    result = home_sum(split_blocks, first_home, slots, 0)
    return home_sum(split_blocks, rest_home, slots, FIRST, result).reshape(-1, features)


def solution(mesh):
    return jax.shard_map(
        body,
        mesh=mesh,
        in_specs=(
            P(("scene", "seq"), None),
            P(("scene", "seq")),
            P(("scene", "seq")),
            P(),
            P(),
            P(),
        ),
        out_specs=P(("scene", "seq"), None),
        check_vma=False,
    )
```

```python
import functools
import math

import jax
import jax.numpy as jnp
from jax import lax
from jax.experimental import pallas as pl
from jax.experimental.pallas import tpu as pltpu
from jax.sharding import PartitionSpec as P

HEADS = 8
REACH = 2
KEY_TILE = 512
QUERY_TILE = 128
ONES_ROWS = 16
QUARTERS = 2
FIRST = 1
LEAST_MASS = 1e-20
MOST_MASS = 1e30
VMEM_BYTES = 62 * 1024 * 1024
BF = jnp.bfloat16
F32 = jnp.float32


def ring_order(count):
    grids = {16: (4, 2, 2), 64: (4, 4, 4)}
    if count not in grids:
        return list(range(count))
    deep, tall, wide = grids[count]
    columns = [(0, x) for x in range(wide)]
    for y in range(1, tall):
        across = range(wide - 1, 0, -1) if y % 2 else range(1, wide)
        columns += [(y, x) for x in across]
    columns += [(y, 0) for y in range(tall - 1, 0, -1)]
    ring = []
    for at, (y, x) in enumerate(columns):
        along = range(deep) if at % 2 == 0 else range(deep - 1, -1, -1)
        ring += [(z * tall + y) * wide + x for z in along]
    return ring


def params(**more):
    return pltpu.CompilerParams(vmem_limit_bytes=VMEM_BYTES, **more)


def each(count, act):
    def step(i, carry):
        act(i)
        return carry

    lax.fori_loop(0, count, step, 0)


def send_kernel(
    order_ref, offsets_ref, places_ref, points_ref, gain_ref, out_ref, slot_ref, told_ref, points_s, normed_s, taken_s, in_sems, out_sems
):
    block_count, length, features = points_s.shape
    shards = places_ref.shape[0]
    capacity = out_ref.shape[0] // shards
    group = 4

    def copy_in(g):
        rows = pl.ds(g * group, group)
        return pltpu.make_async_copy(points_ref.at[rows], points_s.at[rows], in_sems.at[g])

    def copy_out(b):
        return pltpu.make_async_copy(normed_s.at[b], out_ref.at[slot_ref[b]], out_sems.at[b])

    each(block_count // group, lambda g: copy_in(g).start())

    def clear(d):
        taken_s[d] = 0
        for i in range(capacity):
            told_ref[d * capacity + i] = -1

    each(shards, clear)
    for i in range(offsets_ref.shape[0]):
        told_ref[shards * capacity + i] = offsets_ref[i]

    def place(b):
        position = order_ref[b]
        device = places_ref[lax.div(position, block_count)]
        rank = taken_s[device]
        taken_s[device] = rank + 1
        slot_ref[b] = device * capacity + rank
        told_ref[device * capacity + rank] = lax.rem(position, block_count)

    each(block_count, place)

    def normalise(g):
        copy_in(g).wait()
        values = points_s[pl.ds(g * group, group)].astype(F32).reshape(group * length, features)
        centred = values - jnp.mean(values, axis=-1, keepdims=True)
        spread = jnp.mean(jnp.square(centred), axis=-1, keepdims=True)
        result = (centred * lax.rsqrt(spread + 1e-05) * gain_ref[...]).astype(BF)
        normed_s[pl.ds(g * group, group)] = result.reshape(group, length, features)
        for i in range(group):
            copy_out(g * group + i).start()

    each(block_count // group, normalise)
    each(block_count, lambda b: copy_out(b).wait())


def normed_to_send(blocks, order, offsets, norm_gain, ring, capacity):
    block_count, length, features = blocks.shape
    shards = len(ring)
    return pl.pallas_call(
        send_kernel,
        grid_spec=pltpu.PrefetchScalarGridSpec(
            num_scalar_prefetch=3,
            grid=(1,),
            in_specs=[pl.BlockSpec(memory_space=pl.ANY), pl.BlockSpec((1, features), lambda p, *s: (0, 0))],
            out_specs=[pl.BlockSpec(memory_space=pl.ANY)] + [pl.BlockSpec(memory_space=pltpu.SMEM)] * 2,
            scratch_shapes=[
                pltpu.VMEM(blocks.shape, BF),
                pltpu.VMEM(blocks.shape, BF),
                pltpu.SMEM((shards,), jnp.int32),
                pltpu.SemaphoreType.DMA((block_count // 4,)),
                pltpu.SemaphoreType.DMA((block_count,)),
            ],
        ),
        out_shape=[
            jax.ShapeDtypeStruct((shards * capacity, length, features), BF),
            jax.ShapeDtypeStruct((block_count,), jnp.int32),
            jax.ShapeDtypeStruct((shards * capacity + offsets.shape[0],), jnp.int32),
        ],
        compiler_params=params(),
        name="send",
    )(order, offsets, jnp.asarray(ring, jnp.int32), blocks, norm_gain.reshape(1, features))


def sort_kernel(known_ref, ranges_ref, arrived_ref, *refs):
    *out_refs, picked_ref, set_ref, within_ref, held_s, in_sems, out_sems = refs
    patch_count, _, per_patch = held_s.shape[:3]
    half = patch_count // 2
    slot_count = arrived_ref.shape[0]
    entry = slot_count + patch_count
    capacity = slot_count // (known_ref.shape[0] // entry)
    my_place = lax.axis_index("seq")
    my_range = ranges_ref[my_place]

    def copy_in(patch, i):
        at = patch * per_patch + i
        return pltpu.make_async_copy(arrived_ref.at[picked_ref[at]], held_s.at[patch, :, i], in_sems.at[at])

    def copies_out(patch):
        for chunk, quarters in enumerate((slice(0, FIRST), slice(FIRST, QUARTERS))):
            count = quarters.stop - quarters.start
            out_ref = out_refs[2 * chunk + patch // half]
            yield pltpu.make_async_copy(
                held_s.at[patch, pl.ds(quarters.start, count)], out_ref.at[patch % half], out_sems.at[patch, chunk]
            )

    each(patch_count * per_patch, lambda i: picked_ref.__setitem__(i, 0))

    def find(sender):
        for rank in range(capacity):
            position = known_ref[sender * entry + my_place * capacity + rank]

            @pl.when(position >= 0)
            def _():
                picked_ref[position] = sender * capacity + rank

    each(slot_count // capacity, find)
    for patch in range(patch_count):
        for i in range(per_patch):
            copy_in(patch, i).start()
    for patch in range(patch_count):
        wanted = patch + known_ref[my_range * entry + slot_count + patch] + REACH
        set_ref[patch] = lax.div(wanted, half)
        within_ref[patch] = lax.rem(wanted, half)
    for patch in range(patch_count):
        for i in range(per_patch):
            copy_in(patch, i).wait()
        for copy in copies_out(patch):
            copy.start()
    for patch in range(patch_count):
        for copy in copies_out(patch):
            copy.wait()


def sorted_patches(arrived, known, ranges, block_count, patch_count):
    _, quarters, length, features = arrived.shape
    per_patch = block_count // patch_count
    half = patch_count // 2
    patch_shape = (quarters, per_patch, length, features)
    counts = (block_count, patch_count, patch_count)
    chunk_shapes = [(half, count, per_patch, length, features) for count in (FIRST, quarters - FIRST) for _ in range(2)]
    results = pl.pallas_call(
        sort_kernel,
        grid_spec=pltpu.PrefetchScalarGridSpec(
            num_scalar_prefetch=2,
            grid=(1,),
            in_specs=[pl.BlockSpec(memory_space=pl.ANY)],
            out_specs=[pl.BlockSpec(memory_space=pl.ANY)] * 4 + [pl.BlockSpec(memory_space=pltpu.SMEM)] * 3,
            scratch_shapes=[
                pltpu.VMEM((patch_count,) + patch_shape, BF),
                pltpu.SemaphoreType.DMA((block_count,)),
                pltpu.SemaphoreType.DMA((patch_count, 2)),
            ],
        ),
        out_shape=[jax.ShapeDtypeStruct(shape, BF) for shape in chunk_shapes]
        + [jax.ShapeDtypeStruct((count,), jnp.int32) for count in counts],
        compiler_params=params(),
        name="sort",
    )(known, jnp.asarray(ranges, jnp.int32), arrived)
    return [chunk.reshape(-1, features) for chunk in results[:4]], results[4:]


def home_kernel(slot_ref, points_ref, part_ref, *refs, start):
    out_ref, points_s, part_s, out_s, in_sems, out_sems = refs[-6:]
    block_count, quarters = points_s.shape[:2]
    group = block_count // out_sems.shape[0]

    def place(g):
        return pl.ds(g * group, group), pl.ds(start, quarters)

    def copies_in(g):
        sems = in_sems.at[g]
        yield pltpu.make_async_copy(points_ref.at[place(g)], points_s.at[pl.ds(g * group, group)], sems.at[0])
        for i in range(group):
            b = g * group + i
            yield pltpu.make_async_copy(part_ref.at[slot_ref[b]], part_s.at[b], sems.at[1 + i])

    def copy_out(g):
        return pltpu.make_async_copy(out_s.at[pl.ds(g * group, group)], out_ref.at[place(g)], out_sems.at[g])

    def begin(g):
        for copy in copies_in(g):
            copy.start()

    def add(g):
        for copy in copies_in(g):
            copy.wait()
        rows = pl.ds(g * group, group)
        out_s[rows] = (points_s[rows].astype(F32) + part_s[rows].astype(F32)).astype(BF)
        copy_out(g).start()

    each(block_count // group, begin)
    each(block_count // group, add)
    each(block_count // group, lambda g: copy_out(g).wait())


def home_sum(blocks, part, slots, start, result=None):
    block_count = blocks.shape[0]
    group = 4
    chunk_shape = (block_count,) + part.shape[1:]
    operands = (slots, blocks, part) + (() if result is None else (result,))
    return pl.pallas_call(
        functools.partial(home_kernel, start=start),
        grid_spec=pltpu.PrefetchScalarGridSpec(
            num_scalar_prefetch=1,
            grid=(1,),
            in_specs=[pl.BlockSpec(memory_space=pl.ANY)] * (len(operands) - 1),
            out_specs=pl.BlockSpec(memory_space=pl.ANY),
            scratch_shapes=[
                pltpu.VMEM(chunk_shape, BF),
                pltpu.VMEM(chunk_shape, BF),
                pltpu.VMEM(chunk_shape, BF),
                pltpu.SemaphoreType.DMA((block_count // group, 1 + group)),
                pltpu.SemaphoreType.DMA((block_count // group,)),
            ],
        ),
        out_shape=jax.ShapeDtypeStruct(blocks.shape, BF),
        input_output_aliases={} if result is None else {3: 0},
        compiler_params=params(),
        cost_estimate=cost(5),
        name="home",
    )(*operands)


def nt_dot(a, b):
    return lax.dot_general(a, b, (((1,), (1,)), ((), ())), preferred_element_type=F32)


def in_range(mass):
    good = jnp.logical_and(mass >= LEAST_MASS, mass <= MOST_MASS)
    return jnp.min(jnp.where(good, 1.0, 0.0)) > 0.5


def lone_head(pair, which, width):
    kept = pair[which * width : (which + 1) * width]
    blank = jnp.zeros_like(kept)
    return jnp.concatenate([kept, blank] if which == 0 else [blank, kept], axis=0)


def with_ones(values):
    return jnp.concatenate([values, jnp.ones((ONES_ROWS, values.shape[1]), BF)], axis=0)


def plain_pair(query_ref, key_ref, value_ref, pair, width):
    features = slice(2 * pair * width, 2 * (pair + 1) * width)
    queries = query_ref[features, :]
    count = queries.shape[1]
    both = jnp.concatenate([lone_head(queries, which, width) for which in range(2)], axis=1)
    sums = None
    for at in range(0, key_ref.shape[0], KEY_TILE):
        scores = jnp.dot(key_ref[at : at + KEY_TILE, features], both, preferred_element_type=F32)
        raised = jnp.exp(scores).astype(BF)
        values = with_ones(value_ref[features, at : at + KEY_TILE])
        part = jnp.dot(values, raised, preferred_element_type=F32)
        sums = part if sums is None else sums + part
    mass = slice(2 * width, 2 * width + 1)
    return [
        (sums[which * width : (which + 1) * width, columns], sums[mass, columns])
        for which, columns in enumerate((slice(0, count), slice(count, 2 * count)))
    ]


def plain_sums(query_ref, pieces, before, width, emit):
    masses = []
    for pair in range(query_ref.shape[0] // (2 * width)):
        found = [plain_pair(query_ref, key_ref, value_ref, pair, width) for key_ref, value_ref in pieces]
        for head in (2 * pair, 2 * pair + 1):
            rows, one = slice(head * width, (head + 1) * width), slice(head, head + 1)
            total, mass = found[0][head % 2]
            for piece in found[1:]:
                total, mass = total + piece[head % 2][0], mass + piece[head % 2][1]
            if before is not None:
                total, mass = total + before[0][rows, :], mass + before[1][one, :]
            masses.append(mass)
            emit(rows, one, slice(None), total, mass, jnp.zeros_like(mass))
    good = in_range(jnp.concatenate(masses, axis=0))
    if before is not None:
        good = jnp.logical_and(good, jnp.max(jnp.abs(before[2][...])) == 0.0)
    return good


def shifted_sums(query_ref, pieces, before, width, emit):
    def step(tile):
        columns = pl.ds(pl.multiple_of(tile * QUERY_TILE, QUERY_TILE), QUERY_TILE)
        for head in range(query_ref.shape[0] // width):
            rows, one = slice(head * width, (head + 1) * width), slice(head, head + 1)
            pair = 2 * width * (head // 2)
            features = slice(pair, pair + 2 * width)
            query = lone_head(query_ref[features, columns], head % 2, width)
            total = mass = top = None
            if before is not None:
                total, mass, top = before[0][rows, columns], before[1][one, columns], before[2][one, columns]
            for key_ref, value_ref in pieces:
                scores = jnp.dot(key_ref[:, features], query, preferred_element_type=F32)
                highest = jnp.max(scores, axis=0, keepdims=True)
                if top is not None:
                    highest = jnp.maximum(highest, top)
                raised = jnp.exp(scores - highest).astype(BF)
                sums = jnp.dot(with_ones(value_ref[rows, :]), raised, preferred_element_type=F32)
                if top is None:
                    total, mass = sums[:width], sums[width : width + 1]
                else:
                    scale = jnp.exp(top - highest)
                    total, mass = total * scale + sums[:width], mass * scale + sums[width : width + 1]
                top = highest
            emit(rows, one, columns, total, mass, top)

    each(query_ref.shape[1] // QUERY_TILE, step)


def attend(query_ref, pieces, before, emit, finish=None):
    width = query_ref.shape[0] // HEADS
    good = plain_sums(query_ref, pieces, before, width, emit)
    if finish is not None:
        finish()

    @pl.when(jnp.logical_not(good))
    def _():
        shifted_sums(query_ref, pieces, before, width, emit)
        if finish is not None:
            finish()


def keep_in(total_ref, mass_ref, top_ref):
    def emit(rows, one, columns, total, mass, top):
        total_ref[rows, columns] = total
        mass_ref[one, columns] = mass
        top_ref[one, columns] = top

    return emit


def normalise_in(mixed_s):
    def emit(rows, one, columns, total, mass, top):
        mixed_s[rows, columns] = (total * (1.0 / mass)).astype(BF)

    return emit


def projected_out(picked_ref, wo_ref, out_ref, mixed_s):
    _, quarters, length, _ = out_ref.shape
    per_patch = mixed_s.shape[1] // (quarters * length)

    def finish():
        mixed = lax.dot_general(mixed_s[...], wo_ref[...], (((0,), (0,)), ((), ())), preferred_element_type=F32)
        mixed = mixed.astype(BF)
        for i in range(per_patch):
            slot = picked_ref[pl.program_id(0) * per_patch + i]
            for quarter in range(quarters):
                at = (quarter * per_patch + i) * length
                out_ref[slot, quarter] = mixed[at : at + length]

    return finish


def own_kernel(low0_ref, high0_ref, low1_ref, high1_ref, wk_ref, wqv_ref, *refs):
    query0_ref, query1_ref, key_ref, value_ref, *state_refs = refs
    patch = pl.program_id(0)
    half = pl.num_programs(0) // 2
    features = wk_ref.shape[0]

    def project(chunks):
        at = 0
        for normed_ref, query_ref in zip(chunks, (query0_ref, query1_ref)):
            normed = normed_ref[...]
            rows = slice(at, at + normed.shape[0])
            key_ref[rows, :] = jnp.dot(normed, wk_ref[...], preferred_element_type=F32).astype(BF)
            both = nt_dot(wqv_ref[...], normed)
            query_ref[...] = both[:features].astype(BF) * math.sqrt(HEADS / features)
            value_ref[:, rows] = both[features:].astype(BF)
            at = rows.stop

    @pl.when(patch < half)
    def _():
        project((low0_ref, low1_ref))

    @pl.when(patch >= half)
    def _():
        project((high0_ref, high1_ref))

    attend(query0_ref, [(key_ref, value_ref)], None, keep_in(*state_refs))


def along(p, *s):
    return (0, p)


def down(p, *s):
    return (p, 0)


def whole(p, *s):
    return (0, 0)


def cost(microseconds):
    return pl.CostEstimate(flops=microseconds * 10**9, bytes_accessed=28 * 10**6, transcendentals=0)


def split_specs(arrays, patch_count):
    return [pl.BlockSpec((part.shape[0], part.shape[1] // patch_count), along) for part in arrays]


def own_attention(chunks, wk, wqv, patch_count):
    features = wk.shape[0]
    half = patch_count // 2
    counts = [chunk.shape[0] // half for chunk in chunks]
    rows = counts[0] + counts[2]
    shapes = [
        jax.ShapeDtypeStruct((features, patch_count * counts[0]), BF),
        jax.ShapeDtypeStruct((features, patch_count * counts[2]), BF),
        jax.ShapeDtypeStruct((patch_count * rows, features), BF),
        jax.ShapeDtypeStruct((features, patch_count * rows), BF),
        jax.ShapeDtypeStruct((features, patch_count * counts[0]), F32),
        jax.ShapeDtypeStruct((HEADS, patch_count * counts[0]), F32),
        jax.ShapeDtypeStruct((HEADS, patch_count * counts[0]), F32),
    ]
    specs = split_specs(shapes, patch_count)
    specs[2] = pl.BlockSpec((rows, features), down)
    lower = lambda p: (jnp.minimum(p, half - 1), 0)
    upper = lambda p: (jnp.maximum(p - half, 0), 0)
    query0, query1, keys, values, *state = pl.pallas_call(
        own_kernel,
        grid=(patch_count,),
        in_specs=[
            pl.BlockSpec((count, features), upper if i % 2 else lower) for i, count in enumerate(counts)
        ]
        + [pl.BlockSpec(wk.shape, whole), pl.BlockSpec(wqv.shape, whole)],
        out_specs=specs,
        out_shape=shapes,
        compiler_params=params(),
        cost_estimate=cost(26),
        name="own",
    )(*chunks, wk, wqv)
    return query0, query1, keys, values, state


def partner_kernel(picked_ref, source_ref, within_ref, *refs, last):
    set_refs, refs = refs[:4], refs[4:]
    query_ref, *before = refs[:4]
    wk_ref, wv_ref = refs[4:6]
    if last:
        wo_ref, out_ref, key_ref, value_ref, normed_s, sems, mixed_s = refs[6:]
    else:
        key_ref, value_ref, *state_refs, normed_s, sems = refs[6:]
    patch = pl.program_id(0)
    rows = normed_s.shape[1]
    now = lax.rem(patch, 2)

    def copy(set_ref, which, at):
        return pltpu.make_async_copy(set_ref.at[pl.ds(which * rows, rows)], normed_s.at[at], sems.at[at])

    def begin(which):
        for number, set_ref in enumerate(set_refs):

            @pl.when(source_ref[which] == number)
            def _(set_ref=set_ref):
                copy(set_ref, within_ref[which], lax.rem(which, 2)).start()

    @pl.when(patch == 0)
    def _():
        begin(patch)

    @pl.when(patch + 1 < pl.num_programs(0))
    def _():
        begin(patch + 1)

    copy(set_refs[1], 0, now).wait()
    normed = normed_s[now]
    key_ref[...] = jnp.dot(normed, wk_ref[...], preferred_element_type=F32).astype(BF)
    value_ref[...] = nt_dot(wv_ref[...], normed).astype(BF)
    pieces = [(key_ref, value_ref)]
    if last:
        attend(query_ref, pieces, before, normalise_in(mixed_s), projected_out(picked_ref, wo_ref, out_ref, mixed_s))
    else:
        attend(query_ref, pieces, before, keep_in(*state_refs))


def partner_chunk(places, sets, query, state, wk, wqv, wo=None, out_shape=None):
    features = wk.shape[0]
    patch_count = places[1].shape[0]
    rows = sets[0].shape[0] // (patch_count // 2)
    last = wo is not None
    held = (query, *state)
    made = [
        jax.ShapeDtypeStruct((patch_count * rows, features), BF),
        jax.ShapeDtypeStruct((features, patch_count * rows), BF),
    ]
    made_specs = [pl.BlockSpec((rows, features), down), pl.BlockSpec((features, rows), along)]
    weights = (wk, wqv) + ((wo,) if last else ())
    weight_specs = [pl.BlockSpec(wk.shape, whole), pl.BlockSpec(wk.shape, lambda p, *s: (1, 0))]
    scratch = [pltpu.VMEM((2, rows, features), BF), pltpu.SemaphoreType.DMA((2,))]
    if last:
        weight_specs.append(pl.BlockSpec(wo.shape, whole))
        made = [jax.ShapeDtypeStruct(out_shape, BF)] + made
        made_specs = [pl.BlockSpec(out_shape, lambda p, *s: (0, 0, 0, 0))] + made_specs
        scratch.append(pltpu.VMEM((features, query.shape[1] // patch_count), BF))
    else:
        made += [jax.ShapeDtypeStruct(part.shape, part.dtype) for part in state]
        made_specs += split_specs(state, patch_count)
    return pl.pallas_call(
        functools.partial(partner_kernel, last=last),
        grid_spec=pltpu.PrefetchScalarGridSpec(
            num_scalar_prefetch=3,
            grid=(patch_count,),
            in_specs=[pl.BlockSpec(memory_space=pl.ANY)] * 4 + split_specs(held, patch_count) + weight_specs,
            out_specs=made_specs,
            scratch_shapes=scratch,
        ),
        out_shape=made,
        compiler_params=params(),
        cost_estimate=cost(15),
        name="partner_last" if last else "partner_next",
    )(*places, *sets, *held, *weights)


def rest_kernel(picked_ref, query_ref, *refs):
    *piece_refs, wo_ref, out_ref, mixed_s = refs
    pieces = list(zip(piece_refs[::2], piece_refs[1::2]))
    attend(query_ref, pieces, None, normalise_in(mixed_s), projected_out(picked_ref, wo_ref, out_ref, mixed_s))


def rest_attention(picked, query, pieces, wo, out_shape, patch_count):
    features = wo.shape[0]
    piece_specs = []
    for keys, _ in pieces:
        rows = keys.shape[0] // patch_count
        piece_specs += [pl.BlockSpec((rows, features), down), pl.BlockSpec((features, rows), along)]
    return pl.pallas_call(
        rest_kernel,
        grid_spec=pltpu.PrefetchScalarGridSpec(
            num_scalar_prefetch=1,
            grid=(patch_count,),
            in_specs=split_specs((query,), patch_count) + piece_specs + [pl.BlockSpec(wo.shape, whole)],
            out_specs=pl.BlockSpec(out_shape, lambda p, *s: (0, 0, 0, 0)),
            scratch_shapes=[pltpu.VMEM((features, query.shape[1] // patch_count), BF)],
        ),
        out_shape=jax.ShapeDtypeStruct(out_shape, BF),
        compiler_params=params(),
        cost_estimate=cost(38),
        name="rest",
    )(picked, query, *[array for piece in pieces for array in piece], wo)


def told_by_all(told):
    shards = lax.axis_size("seq")
    if shards & (shards - 1):
        return lax.all_gather(told, "seq", tiled=True)
    me = lax.axis_index("seq")
    step = 1
    while step < shards:
        other = lax.ppermute(told, "seq", [(place, place ^ step) for place in range(shards)])
        told = jnp.where((me & step) == 0, jnp.concatenate([told, other]), jnp.concatenate([other, told]))
        step *= 2
    return told


def exchanged(value):
    return lax.all_to_all(value, "seq", split_axis=0, concat_axis=0, tiled=True)


def body(points, order, offsets, norm_gain, w_qkv, w_out):
    features = points.shape[1]
    block_count = order.shape[0]
    block_rows = points.shape[0] // block_count
    patch_count = offsets.shape[0]
    shards = lax.axis_size("seq")
    capacity = (block_count + shards - 1) // shards
    ring = ring_order(shards)
    ring_next = [(ring[e], ring[(e + 1) % shards]) for e in range(shards)]
    ring_before = [(ring[e], ring[e - 1]) for e in range(shards)]
    ranges = [ring.index(place) for place in range(shards)]
    wk = w_qkv[:, features : 2 * features]
    wqv = jnp.concatenate([w_qkv[:, :features], w_qkv[:, 2 * features :]], axis=1).T

    blocks = points.reshape(block_count, block_rows, features)
    outgoing, slots, told = normed_to_send(blocks, order, offsets, norm_gain, ring, capacity)
    arrived = exchanged(outgoing).reshape(-1, QUARTERS, block_rows // QUARTERS, features)
    known = told_by_all(told)
    chunks, places = sorted_patches(arrived, known, ranges, block_count, patch_count)
    sets = []
    for low, high in (chunks[:2], chunks[2:]):
        left = lax.ppermute(high, "seq", ring_next)
        right = lax.ppermute(low, "seq", ring_before)
        sets.append((left, low, high, right))
    query0, query1, keys, values, state = own_attention(chunks, wk, wqv, patch_count)
    slot_count, _, length, _ = arrived.shape
    keys0, values0, *state = partner_chunk(places, sets[0], query0, state, wk, wqv)
    first, keys1, values1 = partner_chunk(
        places, sets[1], query0, state, wk, wqv, w_out, (slot_count, FIRST, length, features)
    )
    first_home = exchanged(first)
    pieces = [(keys, values), (keys0, values0), (keys1, values1)]
    rest = rest_attention(
        places[0], query1, pieces, w_out, (slot_count, QUARTERS - FIRST, length, features), patch_count
    )
    rest, first_home = lax.optimization_barrier((rest, first_home))
    rest_home = exchanged(rest)
    split_blocks = blocks.reshape(block_count, QUARTERS, block_rows // QUARTERS, features)
    result = home_sum(split_blocks, first_home, slots, 0)
    return home_sum(split_blocks, rest_home, slots, FIRST, result).reshape(-1, features)


def solution(mesh):
    return jax.shard_map(
        body,
        mesh=mesh,
        in_specs=(
            P(("scene", "seq"), None),
            P(("scene", "seq")),
            P(("scene", "seq")),
            P(),
            P(),
            P(),
        ),
        out_specs=P(("scene", "seq"), None),
        check_vma=False,
    )
```

```python
import functools
import math

import jax
import jax.numpy as jnp
from jax import lax
from jax.experimental import pallas as pl
from jax.experimental.pallas import tpu as pltpu
from jax.sharding import PartitionSpec as P

HEADS = 8
REACH = 2
KEY_TILE = 512
QUERY_TILE = 128
ONES_ROWS = 16
QUARTERS = 2
FIRST = 1
LEAST_MASS = 1e-20
MOST_MASS = 1e30
VMEM_BYTES = 62 * 1024 * 1024
BF = jnp.bfloat16
F32 = jnp.float32


def ring_order(count):
    grids = {16: (4, 2, 2), 64: (4, 4, 4)}
    if count not in grids:
        return list(range(count))
    deep, tall, wide = grids[count]
    columns = [(0, x) for x in range(wide)]
    for y in range(1, tall):
        across = range(wide - 1, 0, -1) if y % 2 else range(1, wide)
        columns += [(y, x) for x in across]
    columns += [(y, 0) for y in range(tall - 1, 0, -1)]
    ring = []
    for at, (y, x) in enumerate(columns):
        along = range(deep) if at % 2 == 0 else range(deep - 1, -1, -1)
        ring += [(z * tall + y) * wide + x for z in along]
    return ring


def params(**more):
    return pltpu.CompilerParams(vmem_limit_bytes=VMEM_BYTES, **more)


def each(count, act):
    def step(i, carry):
        act(i)
        return carry

    lax.fori_loop(0, count, step, 0)


def send_kernel(
    order_ref, offsets_ref, places_ref, points_ref, gain_ref, out_ref, slot_ref, told_ref, points_s, normed_s, taken_s, in_sems, out_sems
):
    block_count, length, features = points_s.shape
    shards = places_ref.shape[0]
    capacity = out_ref.shape[0] // shards
    group = 4

    def copy_in(g):
        rows = pl.ds(g * group, group)
        return pltpu.make_async_copy(points_ref.at[rows], points_s.at[rows], in_sems.at[g])

    def copy_out(b):
        return pltpu.make_async_copy(normed_s.at[b], out_ref.at[slot_ref[b]], out_sems.at[b])

    each(block_count // group, lambda g: copy_in(g).start())

    def clear(d):
        taken_s[d] = 0
        for i in range(capacity):
            told_ref[d * capacity + i] = -1

    each(shards, clear)
    for i in range(offsets_ref.shape[0]):
        told_ref[shards * capacity + i] = offsets_ref[i]

    def place(b):
        position = order_ref[b]
        device = places_ref[lax.div(position, block_count)]
        rank = taken_s[device]
        taken_s[device] = rank + 1
        slot_ref[b] = device * capacity + rank
        told_ref[device * capacity + rank] = lax.rem(position, block_count)

    each(block_count, place)

    def normalise(g):
        copy_in(g).wait()
        values = points_s[pl.ds(g * group, group)].astype(F32).reshape(group * length, features)
        centred = values - jnp.mean(values, axis=-1, keepdims=True)
        spread = jnp.mean(jnp.square(centred), axis=-1, keepdims=True)
        result = (centred * lax.rsqrt(spread + 1e-05) * gain_ref[...]).astype(BF)
        normed_s[pl.ds(g * group, group)] = result.reshape(group, length, features)
        for i in range(group):
            copy_out(g * group + i).start()

    each(block_count // group, normalise)
    each(block_count, lambda b: copy_out(b).wait())


def normed_to_send(blocks, order, offsets, norm_gain, ring, capacity):
    block_count, length, features = blocks.shape
    shards = len(ring)
    return pl.pallas_call(
        send_kernel,
        grid_spec=pltpu.PrefetchScalarGridSpec(
            num_scalar_prefetch=3,
            grid=(1,),
            in_specs=[pl.BlockSpec(memory_space=pl.ANY), pl.BlockSpec((1, features), lambda p, *s: (0, 0))],
            out_specs=[pl.BlockSpec(memory_space=pl.ANY)] + [pl.BlockSpec(memory_space=pltpu.SMEM)] * 2,
            scratch_shapes=[
                pltpu.VMEM(blocks.shape, BF),
                pltpu.VMEM(blocks.shape, BF),
                pltpu.SMEM((shards,), jnp.int32),
                pltpu.SemaphoreType.DMA((block_count // 4,)),
                pltpu.SemaphoreType.DMA((block_count,)),
            ],
        ),
        out_shape=[
            jax.ShapeDtypeStruct((shards * capacity, length, features), BF),
            jax.ShapeDtypeStruct((block_count,), jnp.int32),
            jax.ShapeDtypeStruct((shards * capacity + offsets.shape[0],), jnp.int32),
        ],
        compiler_params=params(),
        name="send",
    )(order, offsets, jnp.asarray(ring, jnp.int32), blocks, norm_gain.reshape(1, features))


def sort_kernel(known_ref, ranges_ref, arrived_ref, *refs):
    *out_refs, picked_ref, set_ref, within_ref, held_s, in_sems, out_sems = refs
    patch_count, _, per_patch = held_s.shape[:3]
    half = patch_count // 2
    slot_count = arrived_ref.shape[0]
    entry = slot_count + patch_count
    capacity = slot_count // (known_ref.shape[0] // entry)
    my_place = lax.axis_index("seq")
    my_range = ranges_ref[my_place]

    def copy_in(position, slot):
        place = held_s.at[lax.div(position, per_patch), :, lax.rem(position, per_patch)]
        return pltpu.make_async_copy(arrived_ref.at[slot], place, in_sems.at[position])

    def copies_out(patch):
        for chunk, quarters in enumerate((slice(0, FIRST), slice(FIRST, QUARTERS))):
            count = quarters.stop - quarters.start
            out_ref = out_refs[2 * chunk + patch // half]
            yield pltpu.make_async_copy(
                held_s.at[patch, pl.ds(quarters.start, count)], out_ref.at[patch % half], out_sems.at[patch, chunk]
            )

    def find(sender):
        for rank in range(capacity):
            slot = sender * capacity + rank
            position = known_ref[sender * entry + my_place * capacity + rank]

            @pl.when(position >= 0)
            def _():
                copy_in(position, slot).start()
                picked_ref[position] = slot

    each(slot_count // capacity, find)
    for patch in range(patch_count):
        wanted = patch + known_ref[my_range * entry + slot_count + patch] + REACH
        set_ref[patch] = lax.div(wanted, half)
        within_ref[patch] = lax.rem(wanted, half)
    for patch in range(patch_count):
        for i in range(per_patch):
            copy_in(patch * per_patch + i, 0).wait()
        for copy in copies_out(patch):
            copy.start()
    for patch in range(patch_count):
        for copy in copies_out(patch):
            copy.wait()


def sorted_patches(arrived, known, ranges, block_count, patch_count):
    _, quarters, length, features = arrived.shape
    per_patch = block_count // patch_count
    half = patch_count // 2
    patch_shape = (quarters, per_patch, length, features)
    counts = (block_count, patch_count, patch_count)
    chunk_shapes = [(half, count, per_patch, length, features) for count in (FIRST, quarters - FIRST) for _ in range(2)]
    results = pl.pallas_call(
        sort_kernel,
        grid_spec=pltpu.PrefetchScalarGridSpec(
            num_scalar_prefetch=2,
            grid=(1,),
            in_specs=[pl.BlockSpec(memory_space=pl.ANY)],
            out_specs=[pl.BlockSpec(memory_space=pl.ANY)] * 4 + [pl.BlockSpec(memory_space=pltpu.SMEM)] * 3,
            scratch_shapes=[
                pltpu.VMEM((patch_count,) + patch_shape, BF),
                pltpu.SemaphoreType.DMA((block_count,)),
                pltpu.SemaphoreType.DMA((patch_count, 2)),
            ],
        ),
        out_shape=[jax.ShapeDtypeStruct(shape, BF) for shape in chunk_shapes]
        + [jax.ShapeDtypeStruct((count,), jnp.int32) for count in counts],
        compiler_params=params(),
        name="sort",
    )(known, jnp.asarray(ranges, jnp.int32), arrived)
    return [chunk.reshape(-1, features) for chunk in results[:4]], results[4:]


def home_kernel(slot_ref, points_ref, part_ref, *refs, start):
    out_ref, points_s, part_s, out_s, in_sems, out_sems = refs[-6:]
    block_count, quarters = points_s.shape[:2]
    group = block_count // out_sems.shape[0]

    def place(g):
        return pl.ds(g * group, group), pl.ds(start, quarters)

    def copies_in(g):
        sems = in_sems.at[g]
        yield pltpu.make_async_copy(points_ref.at[place(g)], points_s.at[pl.ds(g * group, group)], sems.at[0])
        for i in range(group):
            b = g * group + i
            yield pltpu.make_async_copy(part_ref.at[slot_ref[b]], part_s.at[b], sems.at[1 + i])

    def copy_out(g):
        return pltpu.make_async_copy(out_s.at[pl.ds(g * group, group)], out_ref.at[place(g)], out_sems.at[g])

    def begin(g):
        for copy in copies_in(g):
            copy.start()

    def add(g):
        for copy in copies_in(g):
            copy.wait()
        rows = pl.ds(g * group, group)
        out_s[rows] = (points_s[rows].astype(F32) + part_s[rows].astype(F32)).astype(BF)
        copy_out(g).start()

    each(block_count // group, begin)
    each(block_count // group, add)
    each(block_count // group, lambda g: copy_out(g).wait())


def home_sum(blocks, part, slots, start, result=None):
    block_count = blocks.shape[0]
    group = 4
    chunk_shape = (block_count,) + part.shape[1:]
    operands = (slots, blocks, part) + (() if result is None else (result,))
    return pl.pallas_call(
        functools.partial(home_kernel, start=start),
        grid_spec=pltpu.PrefetchScalarGridSpec(
            num_scalar_prefetch=1,
            grid=(1,),
            in_specs=[pl.BlockSpec(memory_space=pl.ANY)] * (len(operands) - 1),
            out_specs=pl.BlockSpec(memory_space=pl.ANY),
            scratch_shapes=[
                pltpu.VMEM(chunk_shape, BF),
                pltpu.VMEM(chunk_shape, BF),
                pltpu.VMEM(chunk_shape, BF),
                pltpu.SemaphoreType.DMA((block_count // group, 1 + group)),
                pltpu.SemaphoreType.DMA((block_count // group,)),
            ],
        ),
        out_shape=jax.ShapeDtypeStruct(blocks.shape, BF),
        input_output_aliases={} if result is None else {3: 0},
        compiler_params=params(),
        cost_estimate=cost(5),
        name="home",
    )(*operands)


def nt_dot(a, b):
    return lax.dot_general(a, b, (((1,), (1,)), ((), ())), preferred_element_type=F32)


def in_range(mass):
    good = jnp.logical_and(mass >= LEAST_MASS, mass <= MOST_MASS)
    return jnp.min(jnp.where(good, 1.0, 0.0)) > 0.5


def lone_head(pair, which, width):
    kept = pair[which * width : (which + 1) * width]
    blank = jnp.zeros_like(kept)
    return jnp.concatenate([kept, blank] if which == 0 else [blank, kept], axis=0)


def with_ones(values):
    return jnp.concatenate([values, jnp.ones((ONES_ROWS, values.shape[1]), BF)], axis=0)


def plain_pair(query_ref, key_ref, value_ref, pair, width):
    features = slice(2 * pair * width, 2 * (pair + 1) * width)
    queries = query_ref[features, :]
    count = queries.shape[1]
    both = jnp.concatenate([lone_head(queries, which, width) for which in range(2)], axis=1)
    sums = None
    for at in range(0, key_ref.shape[0], KEY_TILE):
        scores = jnp.dot(key_ref[at : at + KEY_TILE, features], both, preferred_element_type=F32)
        raised = jnp.exp(scores).astype(BF)
        values = with_ones(value_ref[features, at : at + KEY_TILE])
        part = jnp.dot(values, raised, preferred_element_type=F32)
        sums = part if sums is None else sums + part
    mass = slice(2 * width, 2 * width + 1)
    return [
        (sums[which * width : (which + 1) * width, columns], sums[mass, columns])
        for which, columns in enumerate((slice(0, count), slice(count, 2 * count)))
    ]


def plain_sums(query_ref, pieces, before, width, emit):
    masses = []
    for pair in range(query_ref.shape[0] // (2 * width)):
        found = [plain_pair(query_ref, key_ref, value_ref, pair, width) for key_ref, value_ref in pieces]
        for head in (2 * pair, 2 * pair + 1):
            rows, one = slice(head * width, (head + 1) * width), slice(head, head + 1)
            total, mass = found[0][head % 2]
            for piece in found[1:]:
                total, mass = total + piece[head % 2][0], mass + piece[head % 2][1]
            if before is not None:
                total, mass = total + before[0][rows, :], mass + before[1][one, :]
            masses.append(mass)
            emit(rows, one, slice(None), total, mass, jnp.zeros_like(mass))
    good = in_range(jnp.concatenate(masses, axis=0))
    if before is not None:
        good = jnp.logical_and(good, jnp.max(jnp.abs(before[2][...])) == 0.0)
    return good


def shifted_sums(query_ref, pieces, before, width, emit):
    def step(tile):
        columns = pl.ds(pl.multiple_of(tile * QUERY_TILE, QUERY_TILE), QUERY_TILE)
        for head in range(query_ref.shape[0] // width):
            rows, one = slice(head * width, (head + 1) * width), slice(head, head + 1)
            pair = 2 * width * (head // 2)
            features = slice(pair, pair + 2 * width)
            query = lone_head(query_ref[features, columns], head % 2, width)
            total = mass = top = None
            if before is not None:
                total, mass, top = before[0][rows, columns], before[1][one, columns], before[2][one, columns]
            for key_ref, value_ref in pieces:
                scores = jnp.dot(key_ref[:, features], query, preferred_element_type=F32)
                highest = jnp.max(scores, axis=0, keepdims=True)
                if top is not None:
                    highest = jnp.maximum(highest, top)
                raised = jnp.exp(scores - highest).astype(BF)
                sums = jnp.dot(with_ones(value_ref[rows, :]), raised, preferred_element_type=F32)
                if top is None:
                    total, mass = sums[:width], sums[width : width + 1]
                else:
                    scale = jnp.exp(top - highest)
                    total, mass = total * scale + sums[:width], mass * scale + sums[width : width + 1]
                top = highest
            emit(rows, one, columns, total, mass, top)

    each(query_ref.shape[1] // QUERY_TILE, step)


def attend(query_ref, pieces, before, emit, finish=None):
    width = query_ref.shape[0] // HEADS
    good = plain_sums(query_ref, pieces, before, width, emit)
    if finish is not None:
        finish()

    @pl.when(jnp.logical_not(good))
    def _():
        shifted_sums(query_ref, pieces, before, width, emit)
        if finish is not None:
            finish()


def keep_in(total_ref, mass_ref, top_ref):
    def emit(rows, one, columns, total, mass, top):
        total_ref[rows, columns] = total
        mass_ref[one, columns] = mass
        top_ref[one, columns] = top

    return emit


def normalise_in(mixed_s):
    def emit(rows, one, columns, total, mass, top):
        mixed_s[rows, columns] = (total * (1.0 / mass)).astype(BF)

    return emit


def projected_out(picked_ref, wo_ref, out_ref, mixed_s):
    _, quarters, length, _ = out_ref.shape
    per_patch = mixed_s.shape[1] // (quarters * length)

    def finish():
        mixed = lax.dot_general(mixed_s[...], wo_ref[...], (((0,), (0,)), ((), ())), preferred_element_type=F32)
        mixed = mixed.astype(BF)
        for i in range(per_patch):
            slot = picked_ref[pl.program_id(0) * per_patch + i]
            for quarter in range(quarters):
                at = (quarter * per_patch + i) * length
                out_ref[slot, quarter] = mixed[at : at + length]

    return finish


def own_kernel(low0_ref, high0_ref, low1_ref, high1_ref, wk_ref, wqv_ref, *refs):
    query0_ref, query1_ref, key_ref, value_ref, *state_refs = refs
    patch = pl.program_id(0)
    half = pl.num_programs(0) // 2
    features = wk_ref.shape[0]

    def project(chunks):
        at = 0
        for normed_ref, query_ref in zip(chunks, (query0_ref, query1_ref)):
            normed = normed_ref[...]
            rows = slice(at, at + normed.shape[0])
            key_ref[rows, :] = jnp.dot(normed, wk_ref[...], preferred_element_type=F32).astype(BF)
            both = nt_dot(wqv_ref[...], normed)
            query_ref[...] = both[:features].astype(BF) * math.sqrt(HEADS / features)
            value_ref[:, rows] = both[features:].astype(BF)
            at = rows.stop

    @pl.when(patch < half)
    def _():
        project((low0_ref, low1_ref))

    @pl.when(patch >= half)
    def _():
        project((high0_ref, high1_ref))

    attend(query0_ref, [(key_ref, value_ref)], None, keep_in(*state_refs))


def along(p, *s):
    return (0, p)


def down(p, *s):
    return (p, 0)


def whole(p, *s):
    return (0, 0)


def cost(microseconds):
    return pl.CostEstimate(flops=microseconds * 10**9, bytes_accessed=28 * 10**6, transcendentals=0)


def split_specs(arrays, patch_count):
    return [pl.BlockSpec((part.shape[0], part.shape[1] // patch_count), along) for part in arrays]


def own_attention(chunks, wk, wqv, patch_count):
    features = wk.shape[0]
    half = patch_count // 2
    counts = [chunk.shape[0] // half for chunk in chunks]
    rows = counts[0] + counts[2]
    shapes = [
        jax.ShapeDtypeStruct((features, patch_count * counts[0]), BF),
        jax.ShapeDtypeStruct((features, patch_count * counts[2]), BF),
        jax.ShapeDtypeStruct((patch_count * rows, features), BF),
        jax.ShapeDtypeStruct((features, patch_count * rows), BF),
        jax.ShapeDtypeStruct((features, patch_count * counts[0]), F32),
        jax.ShapeDtypeStruct((HEADS, patch_count * counts[0]), F32),
        jax.ShapeDtypeStruct((HEADS, patch_count * counts[0]), F32),
    ]
    specs = split_specs(shapes, patch_count)
    specs[2] = pl.BlockSpec((rows, features), down)
    lower = lambda p: (jnp.minimum(p, half - 1), 0)
    upper = lambda p: (jnp.maximum(p - half, 0), 0)
    query0, query1, keys, values, *state = pl.pallas_call(
        own_kernel,
        grid=(patch_count,),
        in_specs=[
            pl.BlockSpec((count, features), upper if i % 2 else lower) for i, count in enumerate(counts)
        ]
        + [pl.BlockSpec(wk.shape, whole), pl.BlockSpec(wqv.shape, whole)],
        out_specs=specs,
        out_shape=shapes,
        compiler_params=params(),
        cost_estimate=cost(26),
        name="own",
    )(*chunks, wk, wqv)
    return query0, query1, keys, values, state


def partner_kernel(picked_ref, source_ref, within_ref, *refs, last):
    set_refs, refs = refs[:4], refs[4:]
    query_ref, *before = refs[:4]
    wk_ref, wv_ref = refs[4:6]
    if last:
        wo_ref, out_ref, key_ref, value_ref, normed_s, sems, mixed_s = refs[6:]
    else:
        key_ref, value_ref, *state_refs, normed_s, sems = refs[6:]
    patch = pl.program_id(0)
    rows = normed_s.shape[1]
    now = lax.rem(patch, 2)

    def copy(set_ref, which, at):
        return pltpu.make_async_copy(set_ref.at[pl.ds(which * rows, rows)], normed_s.at[at], sems.at[at])

    def begin(which):
        for number, set_ref in enumerate(set_refs):

            @pl.when(source_ref[which] == number)
            def _(set_ref=set_ref):
                copy(set_ref, within_ref[which], lax.rem(which, 2)).start()

    @pl.when(patch == 0)
    def _():
        begin(patch)

    @pl.when(patch + 1 < pl.num_programs(0))
    def _():
        begin(patch + 1)

    copy(set_refs[1], 0, now).wait()
    normed = normed_s[now]
    key_ref[...] = jnp.dot(normed, wk_ref[...], preferred_element_type=F32).astype(BF)
    value_ref[...] = nt_dot(wv_ref[...], normed).astype(BF)
    pieces = [(key_ref, value_ref)]
    if last:
        attend(query_ref, pieces, before, normalise_in(mixed_s), projected_out(picked_ref, wo_ref, out_ref, mixed_s))
    else:
        attend(query_ref, pieces, before, keep_in(*state_refs))


def partner_chunk(places, sets, query, state, wk, wqv, wo=None, out_shape=None):
    features = wk.shape[0]
    patch_count = places[1].shape[0]
    rows = sets[0].shape[0] // (patch_count // 2)
    last = wo is not None
    held = (query, *state)
    made = [
        jax.ShapeDtypeStruct((patch_count * rows, features), BF),
        jax.ShapeDtypeStruct((features, patch_count * rows), BF),
    ]
    made_specs = [pl.BlockSpec((rows, features), down), pl.BlockSpec((features, rows), along)]
    weights = (wk, wqv) + ((wo,) if last else ())
    weight_specs = [pl.BlockSpec(wk.shape, whole), pl.BlockSpec(wk.shape, lambda p, *s: (1, 0))]
    scratch = [pltpu.VMEM((2, rows, features), BF), pltpu.SemaphoreType.DMA((2,))]
    if last:
        weight_specs.append(pl.BlockSpec(wo.shape, whole))
        made = [jax.ShapeDtypeStruct(out_shape, BF)] + made
        made_specs = [pl.BlockSpec(out_shape, lambda p, *s: (0, 0, 0, 0))] + made_specs
        scratch.append(pltpu.VMEM((features, query.shape[1] // patch_count), BF))
    else:
        made += [jax.ShapeDtypeStruct(part.shape, part.dtype) for part in state]
        made_specs += split_specs(state, patch_count)
    return pl.pallas_call(
        functools.partial(partner_kernel, last=last),
        grid_spec=pltpu.PrefetchScalarGridSpec(
            num_scalar_prefetch=3,
            grid=(patch_count,),
            in_specs=[pl.BlockSpec(memory_space=pl.ANY)] * 4 + split_specs(held, patch_count) + weight_specs,
            out_specs=made_specs,
            scratch_shapes=scratch,
        ),
        out_shape=made,
        compiler_params=params(),
        cost_estimate=cost(15),
        name="partner_last" if last else "partner_next",
    )(*places, *sets, *held, *weights)


def rest_kernel(picked_ref, query_ref, *refs):
    *piece_refs, wo_ref, out_ref, mixed_s = refs
    pieces = list(zip(piece_refs[::2], piece_refs[1::2]))
    attend(query_ref, pieces, None, normalise_in(mixed_s), projected_out(picked_ref, wo_ref, out_ref, mixed_s))


def rest_attention(picked, query, pieces, wo, out_shape, patch_count):
    features = wo.shape[0]
    piece_specs = []
    for keys, _ in pieces:
        rows = keys.shape[0] // patch_count
        piece_specs += [pl.BlockSpec((rows, features), down), pl.BlockSpec((features, rows), along)]
    return pl.pallas_call(
        rest_kernel,
        grid_spec=pltpu.PrefetchScalarGridSpec(
            num_scalar_prefetch=1,
            grid=(patch_count,),
            in_specs=split_specs((query,), patch_count) + piece_specs + [pl.BlockSpec(wo.shape, whole)],
            out_specs=pl.BlockSpec(out_shape, lambda p, *s: (0, 0, 0, 0)),
            scratch_shapes=[pltpu.VMEM((features, query.shape[1] // patch_count), BF)],
        ),
        out_shape=jax.ShapeDtypeStruct(out_shape, BF),
        compiler_params=params(),
        cost_estimate=cost(38),
        name="rest",
    )(picked, query, *[array for piece in pieces for array in piece], wo)


def told_by_all(told):
    shards = lax.axis_size("seq")
    if shards & (shards - 1):
        return lax.all_gather(told, "seq", tiled=True)
    me = lax.axis_index("seq")
    step = 1
    while step < shards:
        other = lax.ppermute(told, "seq", [(place, place ^ step) for place in range(shards)])
        told = jnp.where((me & step) == 0, jnp.concatenate([told, other]), jnp.concatenate([other, told]))
        step *= 2
    return told


def exchanged(value):
    return lax.all_to_all(value, "seq", split_axis=0, concat_axis=0, tiled=True)


def body(points, order, offsets, norm_gain, w_qkv, w_out):
    features = points.shape[1]
    block_count = order.shape[0]
    block_rows = points.shape[0] // block_count
    patch_count = offsets.shape[0]
    shards = lax.axis_size("seq")
    capacity = (block_count + shards - 1) // shards
    ring = ring_order(shards)
    ring_next = [(ring[e], ring[(e + 1) % shards]) for e in range(shards)]
    ring_before = [(ring[e], ring[e - 1]) for e in range(shards)]
    ranges = [ring.index(place) for place in range(shards)]
    wk = w_qkv[:, features : 2 * features]
    wqv = jnp.concatenate([w_qkv[:, :features], w_qkv[:, 2 * features :]], axis=1).T

    blocks = points.reshape(block_count, block_rows, features)
    outgoing, slots, told = normed_to_send(blocks, order, offsets, norm_gain, ring, capacity)
    arrived = exchanged(outgoing).reshape(-1, QUARTERS, block_rows // QUARTERS, features)
    known = told_by_all(told)
    chunks, places = sorted_patches(arrived, known, ranges, block_count, patch_count)
    sets = []
    for low, high in (chunks[:2], chunks[2:]):
        left = lax.ppermute(high, "seq", ring_next)
        right = lax.ppermute(low, "seq", ring_before)
        sets.append((left, low, high, right))
    query0, query1, keys, values, state = own_attention(chunks, wk, wqv, patch_count)
    slot_count, _, length, _ = arrived.shape
    keys0, values0, *state = partner_chunk(places, sets[0], query0, state, wk, wqv)
    first, keys1, values1 = partner_chunk(
        places, sets[1], query0, state, wk, wqv, w_out, (slot_count, FIRST, length, features)
    )
    first_home = exchanged(first)
    pieces = [(keys, values), (keys0, values0), (keys1, values1)]
    rest = rest_attention(
        places[0], query1, pieces, w_out, (slot_count, QUARTERS - FIRST, length, features), patch_count
    )
    rest, first_home = lax.optimization_barrier((rest, first_home))
    rest_home = exchanged(rest)
    split_blocks = blocks.reshape(block_count, QUARTERS, block_rows // QUARTERS, features)
    result = home_sum(split_blocks, first_home, slots, 0)
    return home_sum(split_blocks, rest_home, slots, FIRST, result).reshape(-1, features)


def solution(mesh):
    return jax.shard_map(
        body,
        mesh=mesh,
        in_specs=(
            P(("scene", "seq"), None),
            P(("scene", "seq")),
            P(("scene", "seq")),
            P(),
            P(),
            P(),
        ),
        out_specs=P(("scene", "seq"), None),
        check_vma=False,
    )
```

```python
import functools
import math

import jax
import jax.numpy as jnp
from jax import lax
from jax.experimental import pallas as pl
from jax.experimental.pallas import tpu as pltpu
from jax.sharding import PartitionSpec as P

HEADS = 8
REACH = 2
KEY_TILE = 512
QUERY_TILE = 128
ONES_ROWS = 16
QUARTERS = 2
FIRST = 1
LEAST_MASS = 1e-20
MOST_MASS = 1e30
VMEM_BYTES = 62 * 1024 * 1024
BF = jnp.bfloat16
F32 = jnp.float32


def ring_order(count):
    grids = {16: (4, 2, 2), 64: (4, 4, 4)}
    if count not in grids:
        return list(range(count))
    deep, tall, wide = grids[count]
    columns = [(0, x) for x in range(wide)]
    for y in range(1, tall):
        across = range(wide - 1, 0, -1) if y % 2 else range(1, wide)
        columns += [(y, x) for x in across]
    columns += [(y, 0) for y in range(tall - 1, 0, -1)]
    ring = []
    for at, (y, x) in enumerate(columns):
        along = range(deep) if at % 2 == 0 else range(deep - 1, -1, -1)
        ring += [(z * tall + y) * wide + x for z in along]
    return ring


def params(**more):
    return pltpu.CompilerParams(vmem_limit_bytes=VMEM_BYTES, **more)


def each(count, act):
    def step(i, carry):
        act(i)
        return carry

    lax.fori_loop(0, count, step, 0)


def send_kernel(
    order_ref, offsets_ref, places_ref, points_ref, gain_ref, out_ref, slot_ref, told_ref, points_s, normed_s, taken_s, in_sems, out_sems
):
    block_count, length, features = points_s.shape
    shards = places_ref.shape[0]
    capacity = out_ref.shape[0] // shards
    group = 4

    def copy_in(g):
        rows = pl.ds(g * group, group)
        return pltpu.make_async_copy(points_ref.at[rows], points_s.at[rows], in_sems.at[g])

    def copy_out(b):
        return pltpu.make_async_copy(normed_s.at[b], out_ref.at[slot_ref[b]], out_sems.at[b])

    each(block_count // group, lambda g: copy_in(g).start())

    def clear(d):
        taken_s[d] = 0
        for i in range(capacity):
            told_ref[d * capacity + i] = -1

    each(shards, clear)
    for i in range(offsets_ref.shape[0]):
        told_ref[shards * capacity + i] = offsets_ref[i]

    def place(b):
        position = order_ref[b]
        device = places_ref[lax.div(position, block_count)]
        rank = taken_s[device]
        taken_s[device] = rank + 1
        slot_ref[b] = device * capacity + rank
        told_ref[device * capacity + rank] = lax.rem(position, block_count)

    each(block_count, place)

    def normalise(g):
        copy_in(g).wait()
        values = points_s[pl.ds(g * group, group)].astype(F32).reshape(group * length, features)
        centred = values - jnp.mean(values, axis=-1, keepdims=True)
        spread = jnp.mean(jnp.square(centred), axis=-1, keepdims=True)
        result = (centred * lax.rsqrt(spread + 1e-05) * gain_ref[...]).astype(BF)
        normed_s[pl.ds(g * group, group)] = result.reshape(group, length, features)
        for i in range(group):
            copy_out(g * group + i).start()

    each(block_count // group, normalise)
    each(block_count, lambda b: copy_out(b).wait())


def normed_to_send(blocks, order, offsets, norm_gain, ring, capacity):
    block_count, length, features = blocks.shape
    shards = len(ring)
    return pl.pallas_call(
        send_kernel,
        grid_spec=pltpu.PrefetchScalarGridSpec(
            num_scalar_prefetch=3,
            grid=(1,),
            in_specs=[pl.BlockSpec(memory_space=pl.ANY), pl.BlockSpec((1, features), lambda p, *s: (0, 0))],
            out_specs=[pl.BlockSpec(memory_space=pl.ANY)] + [pl.BlockSpec(memory_space=pltpu.SMEM)] * 2,
            scratch_shapes=[
                pltpu.VMEM(blocks.shape, BF),
                pltpu.VMEM(blocks.shape, BF),
                pltpu.SMEM((shards,), jnp.int32),
                pltpu.SemaphoreType.DMA((block_count // 4,)),
                pltpu.SemaphoreType.DMA((block_count,)),
            ],
        ),
        out_shape=[
            jax.ShapeDtypeStruct((shards * capacity, length, features), BF),
            jax.ShapeDtypeStruct((block_count,), jnp.int32),
            jax.ShapeDtypeStruct((shards * capacity + offsets.shape[0],), jnp.int32),
        ],
        compiler_params=params(),
        name="send",
    )(order, offsets, jnp.asarray(ring, jnp.int32), blocks, norm_gain.reshape(1, features))


def sort_kernel(known_ref, ranges_ref, arrived_ref, *refs):
    *out_refs, picked_ref, set_ref, within_ref, held_s, in_sems, out_sems = refs
    patch_count, _, per_patch = held_s.shape[:3]
    half = patch_count // 2
    slot_count = arrived_ref.shape[0]
    entry = slot_count + patch_count
    capacity = slot_count // (known_ref.shape[0] // entry)
    my_place = lax.axis_index("seq")
    my_range = ranges_ref[my_place]

    def copy_in(patch, i):
        at = patch * per_patch + i
        return pltpu.make_async_copy(arrived_ref.at[picked_ref[at]], held_s.at[patch, :, i], in_sems.at[at])

    def copies_out(patch):
        for chunk, quarters in enumerate((slice(0, FIRST), slice(FIRST, QUARTERS))):
            count = quarters.stop - quarters.start
            out_ref = out_refs[2 * chunk + patch // half]
            yield pltpu.make_async_copy(
                held_s.at[patch, pl.ds(quarters.start, count)], out_ref.at[patch % half], out_sems.at[patch, chunk]
            )

    each(patch_count * per_patch, lambda i: picked_ref.__setitem__(i, 0))

    def find(sender):
        for rank in range(capacity):
            position = known_ref[sender * entry + my_place * capacity + rank]

            @pl.when(position >= 0)
            def _():
                picked_ref[position] = sender * capacity + rank

    each(slot_count // capacity, find)
    for patch in range(patch_count):
        for i in range(per_patch):
            copy_in(patch, i).start()
    for patch in range(patch_count):
        wanted = patch + known_ref[my_range * entry + slot_count + patch] + REACH
        set_ref[patch] = lax.div(wanted, half)
        within_ref[patch] = lax.rem(wanted, half)
    for patch in range(patch_count):
        for i in range(per_patch):
            copy_in(patch, i).wait()
        for copy in copies_out(patch):
            copy.start()
    for patch in range(patch_count):
        for copy in copies_out(patch):
            copy.wait()


def sorted_patches(arrived, known, ranges, block_count, patch_count):
    _, quarters, length, features = arrived.shape
    per_patch = block_count // patch_count
    half = patch_count // 2
    patch_shape = (quarters, per_patch, length, features)
    counts = (block_count, patch_count, patch_count)
    chunk_shapes = [(half, count, per_patch, length, features) for count in (FIRST, quarters - FIRST) for _ in range(2)]
    results = pl.pallas_call(
        sort_kernel,
        grid_spec=pltpu.PrefetchScalarGridSpec(
            num_scalar_prefetch=2,
            grid=(1,),
            in_specs=[pl.BlockSpec(memory_space=pl.ANY)],
            out_specs=[pl.BlockSpec(memory_space=pl.ANY)] * 4 + [pl.BlockSpec(memory_space=pltpu.SMEM)] * 3,
            scratch_shapes=[
                pltpu.VMEM((patch_count,) + patch_shape, BF),
                pltpu.SemaphoreType.DMA((block_count,)),
                pltpu.SemaphoreType.DMA((patch_count, 2)),
            ],
        ),
        out_shape=[jax.ShapeDtypeStruct(shape, BF) for shape in chunk_shapes]
        + [jax.ShapeDtypeStruct((count,), jnp.int32) for count in counts],
        compiler_params=params(),
        name="sort",
    )(known, jnp.asarray(ranges, jnp.int32), arrived)
    return [chunk.reshape(-1, features) for chunk in results[:4]], results[4:]


def home_kernel(slot_ref, points_ref, part_ref, *refs, start):
    out_ref, points_s, part_s, out_s, in_sems, out_sems = refs[-6:]
    block_count, quarters = points_s.shape[:2]
    group = block_count // out_sems.shape[0]

    def place(g):
        return pl.ds(g * group, group), pl.ds(start, quarters)

    def copies_in(g):
        sems = in_sems.at[g]
        yield pltpu.make_async_copy(points_ref.at[place(g)], points_s.at[pl.ds(g * group, group)], sems.at[0])
        for i in range(group):
            b = g * group + i
            yield pltpu.make_async_copy(part_ref.at[slot_ref[b]], part_s.at[b], sems.at[1 + i])

    def copy_out(g):
        return pltpu.make_async_copy(out_s.at[pl.ds(g * group, group)], out_ref.at[place(g)], out_sems.at[g])

    def begin(g):
        for copy in copies_in(g):
            copy.start()

    def add(g):
        for copy in copies_in(g):
            copy.wait()
        rows = pl.ds(g * group, group)
        out_s[rows] = (points_s[rows].astype(F32) + part_s[rows].astype(F32)).astype(BF)
        copy_out(g).start()

    each(block_count // group, begin)
    each(block_count // group, add)
    each(block_count // group, lambda g: copy_out(g).wait())


def home_sum(blocks, part, slots, start, result=None):
    block_count = blocks.shape[0]
    group = 8
    chunk_shape = (block_count,) + part.shape[1:]
    operands = (slots, blocks, part) + (() if result is None else (result,))
    return pl.pallas_call(
        functools.partial(home_kernel, start=start),
        grid_spec=pltpu.PrefetchScalarGridSpec(
            num_scalar_prefetch=1,
            grid=(1,),
            in_specs=[pl.BlockSpec(memory_space=pl.ANY)] * (len(operands) - 1),
            out_specs=pl.BlockSpec(memory_space=pl.ANY),
            scratch_shapes=[
                pltpu.VMEM(chunk_shape, BF),
                pltpu.VMEM(chunk_shape, BF),
                pltpu.VMEM(chunk_shape, BF),
                pltpu.SemaphoreType.DMA((block_count // group, 1 + group)),
                pltpu.SemaphoreType.DMA((block_count // group,)),
            ],
        ),
        out_shape=jax.ShapeDtypeStruct(blocks.shape, BF),
        input_output_aliases={} if result is None else {3: 0},
        compiler_params=params(),
        cost_estimate=cost(5),
        name="home",
    )(*operands)


def nt_dot(a, b):
    return lax.dot_general(a, b, (((1,), (1,)), ((), ())), preferred_element_type=F32)


def in_range(mass):
    good = jnp.logical_and(mass >= LEAST_MASS, mass <= MOST_MASS)
    return jnp.min(jnp.where(good, 1.0, 0.0)) > 0.5


def lone_head(pair, which, width):
    kept = pair[which * width : (which + 1) * width]
    blank = jnp.zeros_like(kept)
    return jnp.concatenate([kept, blank] if which == 0 else [blank, kept], axis=0)


def with_ones(values):
    return jnp.concatenate([values, jnp.ones((ONES_ROWS, values.shape[1]), BF)], axis=0)


def plain_pair(query_ref, key_ref, value_ref, pair, width):
    features = slice(2 * pair * width, 2 * (pair + 1) * width)
    queries = query_ref[features, :]
    count = queries.shape[1]
    both = jnp.concatenate([lone_head(queries, which, width) for which in range(2)], axis=1)
    sums = None
    for at in range(0, key_ref.shape[0], KEY_TILE):
        scores = jnp.dot(key_ref[at : at + KEY_TILE, features], both, preferred_element_type=F32)
        raised = jnp.exp(scores).astype(BF)
        values = with_ones(value_ref[features, at : at + KEY_TILE])
        part = jnp.dot(values, raised, preferred_element_type=F32)
        sums = part if sums is None else sums + part
    mass = slice(2 * width, 2 * width + 1)
    return [
        (sums[which * width : (which + 1) * width, columns], sums[mass, columns])
        for which, columns in enumerate((slice(0, count), slice(count, 2 * count)))
    ]


def plain_sums(query_ref, pieces, before, width, emit):
    masses = []
    for pair in range(query_ref.shape[0] // (2 * width)):
        found = [plain_pair(query_ref, key_ref, value_ref, pair, width) for key_ref, value_ref in pieces]
        for head in (2 * pair, 2 * pair + 1):
            rows, one = slice(head * width, (head + 1) * width), slice(head, head + 1)
            total, mass = found[0][head % 2]
            for piece in found[1:]:
                total, mass = total + piece[head % 2][0], mass + piece[head % 2][1]
            if before is not None:
                total, mass = total + before[0][rows, :], mass + before[1][one, :]
            masses.append(mass)
            emit(rows, one, slice(None), total, mass, jnp.zeros_like(mass))
    good = in_range(jnp.concatenate(masses, axis=0))
    if before is not None:
        good = jnp.logical_and(good, jnp.max(jnp.abs(before[2][...])) == 0.0)
    return good


def shifted_sums(query_ref, pieces, before, width, emit):
    def step(tile):
        columns = pl.ds(pl.multiple_of(tile * QUERY_TILE, QUERY_TILE), QUERY_TILE)
        for head in range(query_ref.shape[0] // width):
            rows, one = slice(head * width, (head + 1) * width), slice(head, head + 1)
            pair = 2 * width * (head // 2)
            features = slice(pair, pair + 2 * width)
            query = lone_head(query_ref[features, columns], head % 2, width)
            total = mass = top = None
            if before is not None:
                total, mass, top = before[0][rows, columns], before[1][one, columns], before[2][one, columns]
            for key_ref, value_ref in pieces:
                scores = jnp.dot(key_ref[:, features], query, preferred_element_type=F32)
                highest = jnp.max(scores, axis=0, keepdims=True)
                if top is not None:
                    highest = jnp.maximum(highest, top)
                raised = jnp.exp(scores - highest).astype(BF)
                sums = jnp.dot(with_ones(value_ref[rows, :]), raised, preferred_element_type=F32)
                if top is None:
                    total, mass = sums[:width], sums[width : width + 1]
                else:
                    scale = jnp.exp(top - highest)
                    total, mass = total * scale + sums[:width], mass * scale + sums[width : width + 1]
                top = highest
            emit(rows, one, columns, total, mass, top)

    each(query_ref.shape[1] // QUERY_TILE, step)


def attend(query_ref, pieces, before, emit, finish=None):
    width = query_ref.shape[0] // HEADS
    good = plain_sums(query_ref, pieces, before, width, emit)
    if finish is not None:
        finish()

    @pl.when(jnp.logical_not(good))
    def _():
        shifted_sums(query_ref, pieces, before, width, emit)
        if finish is not None:
            finish()


def keep_in(total_ref, mass_ref, top_ref):
    def emit(rows, one, columns, total, mass, top):
        total_ref[rows, columns] = total
        mass_ref[one, columns] = mass
        top_ref[one, columns] = top

    return emit


def normalise_in(mixed_s):
    def emit(rows, one, columns, total, mass, top):
        mixed_s[rows, columns] = (total * (1.0 / mass)).astype(BF)

    return emit


def projected_out(picked_ref, wo_ref, out_ref, mixed_s):
    _, quarters, length, _ = out_ref.shape
    per_patch = mixed_s.shape[1] // (quarters * length)

    def finish():
        mixed = lax.dot_general(mixed_s[...], wo_ref[...], (((0,), (0,)), ((), ())), preferred_element_type=F32)
        mixed = mixed.astype(BF)
        for i in range(per_patch):
            slot = picked_ref[pl.program_id(0) * per_patch + i]
            for quarter in range(quarters):
                at = (quarter * per_patch + i) * length
                out_ref[slot, quarter] = mixed[at : at + length]

    return finish


def own_kernel(low0_ref, high0_ref, low1_ref, high1_ref, wk_ref, wqv_ref, *refs):
    query0_ref, query1_ref, key_ref, value_ref, *state_refs = refs
    patch = pl.program_id(0)
    half = pl.num_programs(0) // 2
    features = wk_ref.shape[0]

    def project(chunks):
        at = 0
        for normed_ref, query_ref in zip(chunks, (query0_ref, query1_ref)):
            normed = normed_ref[...]
            rows = slice(at, at + normed.shape[0])
            key_ref[rows, :] = jnp.dot(normed, wk_ref[...], preferred_element_type=F32).astype(BF)
            both = nt_dot(wqv_ref[...], normed)
            query_ref[...] = both[:features].astype(BF) * math.sqrt(HEADS / features)
            value_ref[:, rows] = both[features:].astype(BF)
            at = rows.stop

    @pl.when(patch < half)
    def _():
        project((low0_ref, low1_ref))

    @pl.when(patch >= half)
    def _():
        project((high0_ref, high1_ref))

    attend(query0_ref, [(key_ref, value_ref)], None, keep_in(*state_refs))


def along(p, *s):
    return (0, p)


def down(p, *s):
    return (p, 0)


def whole(p, *s):
    return (0, 0)


def cost(microseconds):
    return pl.CostEstimate(flops=microseconds * 10**9, bytes_accessed=28 * 10**6, transcendentals=0)


def split_specs(arrays, patch_count):
    return [pl.BlockSpec((part.shape[0], part.shape[1] // patch_count), along) for part in arrays]


def own_attention(chunks, wk, wqv, patch_count):
    features = wk.shape[0]
    half = patch_count // 2
    counts = [chunk.shape[0] // half for chunk in chunks]
    rows = counts[0] + counts[2]
    shapes = [
        jax.ShapeDtypeStruct((features, patch_count * counts[0]), BF),
        jax.ShapeDtypeStruct((features, patch_count * counts[2]), BF),
        jax.ShapeDtypeStruct((patch_count * rows, features), BF),
        jax.ShapeDtypeStruct((features, patch_count * rows), BF),
        jax.ShapeDtypeStruct((features, patch_count * counts[0]), F32),
        jax.ShapeDtypeStruct((HEADS, patch_count * counts[0]), F32),
        jax.ShapeDtypeStruct((HEADS, patch_count * counts[0]), F32),
    ]
    specs = split_specs(shapes, patch_count)
    specs[2] = pl.BlockSpec((rows, features), down)
    lower = lambda p: (jnp.minimum(p, half - 1), 0)
    upper = lambda p: (jnp.maximum(p - half, 0), 0)
    query0, query1, keys, values, *state = pl.pallas_call(
        own_kernel,
        grid=(patch_count,),
        in_specs=[
            pl.BlockSpec((count, features), upper if i % 2 else lower) for i, count in enumerate(counts)
        ]
        + [pl.BlockSpec(wk.shape, whole), pl.BlockSpec(wqv.shape, whole)],
        out_specs=specs,
        out_shape=shapes,
        compiler_params=params(),
        cost_estimate=cost(26),
        name="own",
    )(*chunks, wk, wqv)
    return query0, query1, keys, values, state


def partner_kernel(picked_ref, source_ref, within_ref, *refs, last):
    set_refs, refs = refs[:4], refs[4:]
    query_ref, *before = refs[:4]
    wk_ref, wv_ref = refs[4:6]
    if last:
        wo_ref, out_ref, key_ref, value_ref, normed_s, sems, mixed_s = refs[6:]
    else:
        key_ref, value_ref, *state_refs, normed_s, sems = refs[6:]
    patch = pl.program_id(0)
    rows = normed_s.shape[1]
    now = lax.rem(patch, 2)

    def copy(set_ref, which, at):
        return pltpu.make_async_copy(set_ref.at[pl.ds(which * rows, rows)], normed_s.at[at], sems.at[at])

    def begin(which):
        for number, set_ref in enumerate(set_refs):

            @pl.when(source_ref[which] == number)
            def _(set_ref=set_ref):
                copy(set_ref, within_ref[which], lax.rem(which, 2)).start()

    @pl.when(patch == 0)
    def _():
        begin(patch)

    @pl.when(patch + 1 < pl.num_programs(0))
    def _():
        begin(patch + 1)

    copy(set_refs[1], 0, now).wait()
    normed = normed_s[now]
    key_ref[...] = jnp.dot(normed, wk_ref[...], preferred_element_type=F32).astype(BF)
    value_ref[...] = nt_dot(wv_ref[...], normed).astype(BF)
    pieces = [(key_ref, value_ref)]
    if last:
        attend(query_ref, pieces, before, normalise_in(mixed_s), projected_out(picked_ref, wo_ref, out_ref, mixed_s))
    else:
        attend(query_ref, pieces, before, keep_in(*state_refs))


def partner_chunk(places, sets, query, state, wk, wqv, wo=None, out_shape=None):
    features = wk.shape[0]
    patch_count = places[1].shape[0]
    rows = sets[0].shape[0] // (patch_count // 2)
    last = wo is not None
    held = (query, *state)
    made = [
        jax.ShapeDtypeStruct((patch_count * rows, features), BF),
        jax.ShapeDtypeStruct((features, patch_count * rows), BF),
    ]
    made_specs = [pl.BlockSpec((rows, features), down), pl.BlockSpec((features, rows), along)]
    weights = (wk, wqv) + ((wo,) if last else ())
    weight_specs = [pl.BlockSpec(wk.shape, whole), pl.BlockSpec(wk.shape, lambda p, *s: (1, 0))]
    scratch = [pltpu.VMEM((2, rows, features), BF), pltpu.SemaphoreType.DMA((2,))]
    if last:
        weight_specs.append(pl.BlockSpec(wo.shape, whole))
        made = [jax.ShapeDtypeStruct(out_shape, BF)] + made
        made_specs = [pl.BlockSpec(out_shape, lambda p, *s: (0, 0, 0, 0))] + made_specs
        scratch.append(pltpu.VMEM((features, query.shape[1] // patch_count), BF))
    else:
        made += [jax.ShapeDtypeStruct(part.shape, part.dtype) for part in state]
        made_specs += split_specs(state, patch_count)
    return pl.pallas_call(
        functools.partial(partner_kernel, last=last),
        grid_spec=pltpu.PrefetchScalarGridSpec(
            num_scalar_prefetch=3,
            grid=(patch_count,),
            in_specs=[pl.BlockSpec(memory_space=pl.ANY)] * 4 + split_specs(held, patch_count) + weight_specs,
            out_specs=made_specs,
            scratch_shapes=scratch,
        ),
        out_shape=made,
        compiler_params=params(),
        cost_estimate=cost(15),
        name="partner_last" if last else "partner_next",
    )(*places, *sets, *held, *weights)


def rest_kernel(picked_ref, query_ref, *refs):
    *piece_refs, wo_ref, out_ref, mixed_s = refs
    pieces = list(zip(piece_refs[::2], piece_refs[1::2]))
    attend(query_ref, pieces, None, normalise_in(mixed_s), projected_out(picked_ref, wo_ref, out_ref, mixed_s))


def rest_attention(picked, query, pieces, wo, out_shape, patch_count):
    features = wo.shape[0]
    piece_specs = []
    for keys, _ in pieces:
        rows = keys.shape[0] // patch_count
        piece_specs += [pl.BlockSpec((rows, features), down), pl.BlockSpec((features, rows), along)]
    return pl.pallas_call(
        rest_kernel,
        grid_spec=pltpu.PrefetchScalarGridSpec(
            num_scalar_prefetch=1,
            grid=(patch_count,),
            in_specs=split_specs((query,), patch_count) + piece_specs + [pl.BlockSpec(wo.shape, whole)],
            out_specs=pl.BlockSpec(out_shape, lambda p, *s: (0, 0, 0, 0)),
            scratch_shapes=[pltpu.VMEM((features, query.shape[1] // patch_count), BF)],
        ),
        out_shape=jax.ShapeDtypeStruct(out_shape, BF),
        compiler_params=params(),
        cost_estimate=cost(38),
        name="rest",
    )(picked, query, *[array for piece in pieces for array in piece], wo)


def told_by_all(told):
    shards = lax.axis_size("seq")
    if shards & (shards - 1):
        return lax.all_gather(told, "seq", tiled=True)
    me = lax.axis_index("seq")
    step = 1
    while step < shards:
        other = lax.ppermute(told, "seq", [(place, place ^ step) for place in range(shards)])
        told = jnp.where((me & step) == 0, jnp.concatenate([told, other]), jnp.concatenate([other, told]))
        step *= 2
    return told


def exchanged(value):
    return lax.all_to_all(value, "seq", split_axis=0, concat_axis=0, tiled=True)


def body(points, order, offsets, norm_gain, w_qkv, w_out):
    features = points.shape[1]
    block_count = order.shape[0]
    block_rows = points.shape[0] // block_count
    patch_count = offsets.shape[0]
    shards = lax.axis_size("seq")
    capacity = (block_count + shards - 1) // shards
    ring = ring_order(shards)
    ring_next = [(ring[e], ring[(e + 1) % shards]) for e in range(shards)]
    ring_before = [(ring[e], ring[e - 1]) for e in range(shards)]
    ranges = [ring.index(place) for place in range(shards)]
    wk = w_qkv[:, features : 2 * features]
    wqv = jnp.concatenate([w_qkv[:, :features], w_qkv[:, 2 * features :]], axis=1).T

    blocks = points.reshape(block_count, block_rows, features)
    outgoing, slots, told = normed_to_send(blocks, order, offsets, norm_gain, ring, capacity)
    arrived = exchanged(outgoing).reshape(-1, QUARTERS, block_rows // QUARTERS, features)
    known = told_by_all(told)
    chunks, places = sorted_patches(arrived, known, ranges, block_count, patch_count)
    sets = []
    for low, high in (chunks[:2], chunks[2:]):
        left = lax.ppermute(high, "seq", ring_next)
        right = lax.ppermute(low, "seq", ring_before)
        sets.append((left, low, high, right))
    query0, query1, keys, values, state = own_attention(chunks, wk, wqv, patch_count)
    slot_count, _, length, _ = arrived.shape
    keys0, values0, *state = partner_chunk(places, sets[0], query0, state, wk, wqv)
    first, keys1, values1 = partner_chunk(
        places, sets[1], query0, state, wk, wqv, w_out, (slot_count, FIRST, length, features)
    )
    first_home = exchanged(first)
    pieces = [(keys, values), (keys0, values0), (keys1, values1)]
    rest = rest_attention(
        places[0], query1, pieces, w_out, (slot_count, QUARTERS - FIRST, length, features), patch_count
    )
    rest, first_home = lax.optimization_barrier((rest, first_home))
    rest_home = exchanged(rest)
    split_blocks = blocks.reshape(block_count, QUARTERS, block_rows // QUARTERS, features)
    result = home_sum(split_blocks, first_home, slots, 0)
    return home_sum(split_blocks, rest_home, slots, FIRST, result).reshape(-1, features)


def solution(mesh):
    return jax.shard_map(
        body,
        mesh=mesh,
        in_specs=(
            P(("scene", "seq"), None),
            P(("scene", "seq")),
            P(("scene", "seq")),
            P(),
            P(),
            P(),
        ),
        out_specs=P(("scene", "seq"), None),
        check_vma=False,
    )
```
